32 devices in a mesh: line: 4 (over y, x), tile: 8 (over z, core).
Axes of the slice: x: 2, y: 2, z: 4, core: 2. Of those that a mesh axis runs over, the one named last changes fastest.
Arguments:
- forcing: float32 [10, 64, 8, 512], P(None, None, 'tile', 'line'), may hold values from -1100 to 1100
- block_inverse: float32 [10, 10, 8, 512], P(None, None, 'tile', 'line'), may hold values from -0.8 to 1
- wall_rates: float32 [2, 10, 8, 512], P(None, None, 'tile', 'line'), may hold values from 0 to 1, as said below
- span_couple: float32 [10], replicated, may hold values from 0.1 to 0.4
Outputs:
- basis: float32 [10, 64, 8, 512], P(None, None, 'tile', 'line')
The draws below stay inside these ranges and needn't reach their ends.
Inputs may be any that keep to these rules, and one draw needn't show every extreme that they name: `wall_rates`: every entry lies strictly between 0 and 1.
All inputs are finite; a program needn't handle non-finite values.
Results may differ from the reference program's by a relative error of at most 0.00022.
Values sent between devices are 32-bit elements; how exact they have to be, the bound alone decides.
A program may use at most 64 MiB of HBM per device.

```python
import math
import jax
import jax.numpy as jnp
from jax import lax

VOLUME_VARIABLES = 10
NF = 64
LD = 128
NORMAL_NODES = 512
LATERAL_NODES = 8


def draw_forcing(key, part):
    generator_seeds = jax.random.split(key, 3)
    shape_full = (VOLUME_VARIABLES, NF, LATERAL_NODES, NORMAL_NODES)
    base = jax.random.truncated_normal(generator_seeds[0], -6.0, 6.0, shape_full, jnp.float32)
    comp_scale = jnp.exp(jax.random.uniform(generator_seeds[1], (VOLUME_VARIABLES, 1, 1, 1), jnp.float32, 0.0, math.log(10.0)))
    column_scale = jnp.exp(jax.random.uniform(generator_seeds[2], (1, NF, 1, 1), jnp.float32, 0.0, math.log(2.0)))
    station = 3.0 ** (jnp.arange(LATERAL_NODES, dtype=jnp.float32) / LATERAL_NODES)
    height = 3.0 ** (1.0 - jnp.arange(NORMAL_NODES, dtype=jnp.float32) / NORMAL_NODES)
    return base * comp_scale * column_scale * station[None, None, :, None] * height[None, None, None, :]


def draw_block_inverse(key, part):
    generator_seeds = jax.random.split(key, 2)
    diagonal = jax.random.uniform(generator_seeds[0], (VOLUME_VARIABLES, 1, LATERAL_NODES, NORMAL_NODES), jnp.float32, 0.5, 1.0)
    offside = 0.2 * jax.random.truncated_normal(generator_seeds[1], -4.0, 4.0, (VOLUME_VARIABLES, VOLUME_VARIABLES, LATERAL_NODES, NORMAL_NODES), jnp.float32)
    unit = jnp.eye(VOLUME_VARIABLES, dtype=jnp.float32)[:, :, None, None]
    return offside * (1.0 - unit) + unit * diagonal


def draw_wall_rates(key, part):
    generator_seeds = jax.random.split(key, 7)
    slow_count = 5
    order = jnp.stack([jax.random.permutation(jax.random.fold_in(generator_seeds[0], 0), VOLUME_VARIABLES), jax.random.permutation(jax.random.fold_in(generator_seeds[0], 1), VOLUME_VARIABLES)])
    slow = order < slow_count
    slow_length = NORMAL_NODES * jax.random.uniform(generator_seeds[1], (2, VOLUME_VARIABLES), jnp.float32, 1.5, 4.0)
    fast_length = LD * jax.random.uniform(generator_seeds[2], (2, VOLUME_VARIABLES), jnp.float32, 0.25, 0.4)
    length = jnp.where(slow, slow_length, fast_length)
    phase = jax.random.uniform(generator_seeds[3], (2, VOLUME_VARIABLES), jnp.float32, 0.0, 2.0 * math.pi)
    position = jnp.arange(NORMAL_NODES, dtype=jnp.float32) / NORMAL_NODES
    profile = 2.0 ** jnp.sin(2.0 * math.pi * position[None, None, :] + phase[:, :, None])
    rough = jnp.exp(jax.random.uniform(generator_seeds[4], (2, VOLUME_VARIABLES, LATERAL_NODES, NORMAL_NODES), jnp.float32, math.log(0.7), math.log(1.4)))
    rate = profile[:, :, None, :] * rough / length[:, :, None, None]
    survival_fraction = jnp.exp(-rate)
    excitation_batch = jax.random.bernoulli(generator_seeds[5], 3.0 / NORMAL_NODES, (2, VOLUME_VARIABLES, LATERAL_NODES, NORMAL_NODES))
    relaxation_passes = jax.random.uniform(generator_seeds[6], (2, VOLUME_VARIABLES, LATERAL_NODES, NORMAL_NODES), jnp.float32, 0.5, 0.8)
    return jnp.where(excitation_batch, survival_fraction * relaxation_passes, survival_fraction)


def setup_inputs(seed: int = 0) -> dict:
    arg_keys = jax.random.split(jax.random.key(seed), 5)
    forcing = draw_forcing(jax.random.fold_in(arg_keys[4], 71), 0)
    block_inverse = draw_block_inverse(jax.random.fold_in(arg_keys[4], 71), 0)
    wall_rates = draw_wall_rates(jax.random.fold_in(arg_keys[4], 71), 0)
    span_couple = jnp.clip(jnp.exp(jax.random.uniform(arg_keys[3], (VOLUME_VARIABLES,), jnp.float32, math.log(0.1), math.log(0.4))), 0.1, 0.4)
    return dict(forcing=forcing, block_inverse=block_inverse, wall_rates=wall_rates, span_couple=span_couple)


def apply_block(blocks, values_in):
    return jnp.einsum('kmzj,mrzj->krzj', blocks, values_in, precision=lax.Precision.HIGHEST)

def span_pair(values_in):
    return jnp.roll(values_in, 1, axis=2) + jnp.roll(values_in, -1, axis=2)

def line_solve(survival_fraction, source, backward):
    rates_first = jnp.moveaxis(survival_fraction, -1, 0)
    source_first = jnp.moveaxis(source, -1, 0)

    def advance(state, inputs):
        rate_now, source_now = inputs
        state = rate_now[:, None, :] * state + source_now
        return (state, state)
    _, states = lax.scan(advance, jnp.zeros_like(source[..., 0]), (rates_first, source_first), reverse=backward)
    return jnp.moveaxis(states, 0, -1)

def reference(forcing, block_inverse, wall_rates, span_couple):
    coupling = span_couple[:, None, None, None]
    rise_rate = wall_rates[0]
    fall_rate = wall_rates[1]
    start_field = apply_block(block_inverse, forcing)
    zero_row = jnp.zeros_like(forcing[..., :1])
    above_row = jnp.concatenate([start_field[..., 1:], zero_row], axis=-1)
    source_one = apply_block(block_inverse, forcing + coupling * span_pair(start_field)) + fall_rate[:, None] * above_row
    rising = line_solve(rise_rate, source_one, False)
    below_row = jnp.concatenate([zero_row, rising[..., :-1]], axis=-1)
    source_two = apply_block(block_inverse, forcing + coupling * span_pair(rising)) + rise_rate[:, None] * below_row
    falling = line_solve(fall_rate, source_two, True)
    gram = jnp.einsum('krzj,kszj->rs', falling, falling, precision=lax.Precision.HIGHEST)
    upper_factor = jnp.linalg.cholesky(gram).T
    identity_matrix = jnp.eye(NF, dtype=gram.dtype)
    inverse_factor = jax.scipy.linalg.solve_triangular(upper_factor, identity_matrix, lower=False)
    scale_value = math.sqrt(VOLUME_VARIABLES * LATERAL_NODES * NORMAL_NODES)
    return jnp.einsum('krzj,rs->kszj', falling, inverse_factor, precision=lax.Precision.HIGHEST) * scale_value
```

```python
import functools
import math

import jax
import jax.numpy as jnp
from jax import lax
from jax.experimental import pallas as pl
from jax.experimental.pallas import tpu as pltpu
from jax.sharding import PartitionSpec as P

MESH = pl.DeviceIdType.MESH
ROWS = 8


def reduce_phases(n_line, n_tile):
    pair = 2 if n_tile % 2 == 0 else 1
    phases = [(1, pair, True)]
    stride, rest = pair, n_tile // pair
    while rest > 1:
        factor = 4 if rest % 4 == 0 else next(f for f in range(2, rest + 1) if rest % f == 0)
        phases.append((stride, factor, False))
        stride, rest = stride * factor, rest // factor
    return phases


def phase_peers(phase, n_line):
    stride, factor, with_line = phase
    lines = n_line if with_line else 1
    return [(a, b) for a in range(lines) for b in range(factor) if (a, b) != (0, 0)]


def peer_id(phase, step, n_line):
    stride, factor, _ = phase
    line, tile = lax.axis_index("line"), lax.axis_index("tile")
    digit = lax.rem(lax.div(tile, stride), factor)
    there = lax.rem(digit + step[1], factor)
    return (lax.rem(line + step[0], n_line), tile + (there - digit) * stride)


def split(value):
    high = value.astype(jnp.bfloat16)
    low = (value - high.astype(jnp.float32)).astype(jnp.bfloat16)
    return high, low


def eliminate(gram):
    n = gram.shape[0]
    row = lax.broadcasted_iota(jnp.int32, (n, n), 0)
    col = lax.broadcasted_iota(jnp.int32, (n, n), 1)
    both = jnp.concatenate([gram, (row == col).astype(jnp.float32)], axis=1)
    blocks = [both[v * ROWS : (v + 1) * ROWS] for v in range(n // ROWS)]
    shape = (ROWS, 2 * n)
    sub = lax.broadcasted_iota(jnp.int32, shape, 0)
    scales = []
    for q in range(n // ROWS):
        live = range(q, n // ROWS)
        cols = [
            {v: jnp.broadcast_to(blocks[v][:, ROWS * q + c : ROWS * q + c + 1], shape) for v in live}
            for c in range(ROWS)
        ]
        scale = jnp.zeros(shape, jnp.float32)
        for c in range(ROWS):
            pivot = jnp.broadcast_to(cols[c][q][c : c + 1], shape)
            inv = 1.0 / pivot
            scale = jnp.where(sub == c, lax.rsqrt(pivot), scale)
            factor = {v: cols[c][v] * inv for v in live}
            factor[q] = jnp.where(sub > c, factor[q], 0.0)
            top = jnp.broadcast_to(blocks[q][c : c + 1], shape)
            tops = [jnp.broadcast_to(cols[e][q][c : c + 1], shape) for e in range(c + 1, ROWS)]
            for v in live:
                blocks[v] = blocks[v] - factor[v] * top
                for e in range(c + 1, ROWS):
                    cols[e][v] = cols[e][v] - factor[v] * tops[e - c - 1]
        scales.append(scale)
    return jnp.concatenate([b * s for b, s in zip(blocks, scales)], axis=0)[:, n:]


def kernel(
    n_line, n_tile, n_chunk, phases, scale_value,
    f_ref, a_ref, w_ref, s_ref, o_ref,
    start, z_low, z_high, rise, y_low, y_high, fall,
    edge_out, edge_in, ends_out, ends_in, enter, rates_out, rates_in, steps, whole,
    gram_out, gram_in, halo_send, halo_recv, edge_send, edge_recv, ends_send, ends_recv,
    rates_send, rates_recv, gram_send, gram_recv,
):
    n_comp, n_cols, n_point = f_ref.shape
    wide = n_cols // n_chunk
    line, tile = lax.axis_index("line"), lax.axis_index("tile")
    above, below = lax.rem(tile + 1, n_tile), lax.rem(tile + n_tile - 1, n_tile)
    line_peers = [(lax.rem(line + d, n_line), tile) for d in range(1, n_line)]
    lower_line = (lax.rem(line + n_line - 1, n_line), tile)
    gram_peers = [[peer_id(ph, step, n_line) for step in phase_peers(ph, n_line)] for ph in phases]

    greet = [(line, above), (line, below)] + [p for peers in gram_peers for p in peers]
    barrier = pltpu.get_barrier_semaphore()
    for peer in greet:
        pl.semaphore_signal(barrier, inc=1, device_id=peer, device_id_type=MESH)

    started = []

    def send(src, dst, send_sem, recv_sem, peer):
        copy = pltpu.make_async_remote_copy(
            src_ref=src, dst_ref=dst, send_sem=send_sem, recv_sem=recv_sem,
            device_id=peer, device_id_type=MESH,
        )
        copy.start()
        started.append(copy)
        return copy

    def cut(c):
        return pl.ds(c * wide, wide)

    lane3 = lax.broadcasted_iota(jnp.int32, (n_comp, 1, n_point), 2)
    lane = lax.broadcasted_iota(jnp.int32, (wide, n_point), 1)
    lane8 = lax.broadcasted_iota(jnp.int32, (ROWS, n_point), 1)
    lane_big = lax.broadcasted_iota(jnp.int32, (n_comp, wide, n_point), 2)
    n_steps = (n_point - 1).bit_length()

    def turn(value, by):
        flat = value.reshape(-1, n_point)
        return pltpu.roll(flat, by % n_point, 1).reshape(value.shape)

    def apply_block(value):
        total = a_ref[:, 0] * value[0][None]
        for m in range(1, n_comp):
            total = total + a_ref[:, m] * value[m][None]
        return total

    def pack(value, at):
        packed = jnp.zeros((value.shape[1], n_point), jnp.float32)
        places = lax.broadcasted_iota(jnp.int32, packed.shape, 1)
        for k in range(n_comp):
            packed = jnp.where(places == k, value[k][:, at : at + 1], packed)
        return packed

    def spread(packed):
        return jnp.stack(
            [jnp.broadcast_to(packed[:, k : k + 1], (wide, n_point)) for k in range(n_comp)], axis=0
        )

    def sweep(value, side):
        for i in range(n_steps):
            by = 1 << i
            value = value + steps[side, i] * turn(value, -by if side else by)
        return value

    halos = {}
    edges, ends, rates = [], {}, []

    def send_halo(which, c, field, low, high):
        halos[which, c] = [
            send(field.at[:, cut(c)], low.at[:, cut(c)], halo_send.at[which, c, 0],
                 halo_recv.at[which, c, 0], (line, above)),
            send(field.at[:, cut(c)], high.at[:, cut(c)], halo_send.at[which, c, 1],
                 halo_recv.at[which, c, 1], (line, below)),
        ]

    def send_ends(which, c):
        ends[which, c] = [
            send(ends_out.at[which, cut(c)], ends_in.at[which, d, cut(c)], ends_send.at[which, c, d],
                 ends_recv.at[which, c, d], peer)
            for d, peer in enumerate(line_peers)
        ]

    for c in range(n_chunk):
        field = apply_block(f_ref[:, c * wide : (c + 1) * wide])
        start[:, cut(c)] = field
        edge_out[cut(c)] = pack(field, 0)
        if c == 0:
            pl.semaphore_wait(barrier, len(greet))
        send_halo(0, c, start, z_low, z_high)
        edges.append(
            send(edge_out.at[cut(c)], edge_in.at[cut(c)], edge_send.at[c], edge_recv.at[c], lower_line)
        )

    for side in range(2):
        rate = w_ref[side]
        for i in range(n_steps):
            by = 1 << i
            inside = lane3 < n_point - by if side else lane3 >= by
            steps[side, i] = jnp.where(inside, rate, 0.0)
            rate = rate * jnp.where(inside, turn(rate, -by if side else by), 1.0)
        whole[side] = rate
        at = 0 if side else n_point - 1
        total = jnp.zeros((ROWS, n_point), jnp.float32)
        for k in range(n_comp):
            total = jnp.where(lane8 == k, rate[k][:, at : at + 1], total)
        rates_out[side] = total
    for d, peer in enumerate(line_peers):
        rates.append(send(rates_out, rates_in.at[d], rates_send.at[d], rates_recv.at[d], peer))

    def coupled(c, low, high):
        beside = low[:, c * wide : (c + 1) * wide] + high[:, c * wide : (c + 1) * wide]
        return jnp.stack(
            [f_ref[k, c * wide : (c + 1) * wide] + s_ref[k] * beside[k] for k in range(n_comp)], axis=0
        )

    def entry(which, c):
        for copy in ends[which, c]:
            copy.wait_recv()
        total = jnp.zeros((wide, n_point), jnp.float32)
        carried = jnp.ones((1, n_point), jnp.float32)
        for d in range(1, n_line):
            slot = n_line - d - 1 if which else d - 1
            reached = (line + d < n_line) if which else (line >= d)
            reached = reached.astype(jnp.float32)
            total = total + (carried * reached) * ends_in[which, slot, cut(c)]
            carried = carried * rates_in[slot, which, 0:1]
        return total

    def first(c):
        for copy in halos[0, c] + [edges[c]]:
            copy.wait_recv()
        source = apply_block(coupled(c, z_low, z_high))
        last = (line < n_line - 1).astype(jnp.float32)
        over = jnp.where(
            lane_big == n_point - 1, spread(edge_in[cut(c)] * last),
            turn(start[:, c * wide : (c + 1) * wide], -1),
        )
        value = sweep(source + w_ref[1] * over, 0)
        rise[:, cut(c)] = value
        ends_out[0, cut(c)] = pack(value, n_point - 1)
        send_ends(0, c)

    def first_entry(c):
        if c == 0:
            for copy in rates:
                copy.wait_recv()
        total = entry(0, c)
        enter[cut(c)] = total
        rise[:, cut(c)] = rise[:, cut(c)] + whole[0] * spread(total)
        send_halo(1, c, rise, y_low, y_high)

    def second(c):
        for copy in halos[1, c]:
            copy.wait_recv()
        source = apply_block(coupled(c, y_low, y_high))
        under = jnp.where(
            lane_big == 0, spread(enter[cut(c)]), turn(rise[:, c * wide : (c + 1) * wide], 1)
        )
        value = sweep(source + w_ref[0] * under, 1)
        fall[:, cut(c)] = value
        ends_out[1, cut(c)] = pack(value, 0)
        send_ends(1, c)

    def second_entry(c):
        fall[:, cut(c)] = fall[:, cut(c)] + whole[1] * spread(entry(1, c))

    for work, finish in ((first, first_entry), (second, second_entry)):
        for c in range(n_chunk):
            work(c)
            if c:
                finish(c - 1)
        finish(n_chunk - 1)

    total = jnp.zeros((2 * n_cols, 2 * n_cols), jnp.float32)
    for k in range(n_comp):
        both = jnp.concatenate(split(fall[k]), axis=0)
        total = total + lax.dot_general(
            both, both, (((1,), (1,)), ((), ())), preferred_element_type=jnp.float32
        )
    gram = total[:n_cols] + total[n_cols:]
    gram = gram[:, :n_cols] + gram[:, n_cols:]
    half = n_cols // 2
    packed = jnp.concatenate([gram[:half], gram[half:]], axis=1)
    slot = 0
    for i, peers in enumerate(gram_peers):
        gram_out[i] = packed
        copies = []
        for peer in peers:
            copies.append(
                send(gram_out.at[i], gram_in.at[slot], gram_send.at[slot], gram_recv.at[slot], peer)
            )
            slot += 1
        for j, copy in enumerate(copies):
            copy.wait_recv()
            packed = packed + gram_in[slot - len(copies) + j]
    gram = jnp.concatenate([packed[:, :n_cols], packed[:, n_cols:]], axis=0)

    high, low = split(eliminate(gram) * scale_value)
    left = jnp.concatenate([high, high, low], axis=1)
    for k in range(n_comp):
        top, rest = split(fall[k])
        o_ref[k] = jnp.dot(
            left, jnp.concatenate([top, rest, top], axis=0), preferred_element_type=jnp.float32
        )
    for copy in started:
        copy.wait_send()


def local(n_line, n_tile, forcing, block_inverse, wall_rates, span_couple):
    n_comp, n_cols, n_station, n_point = forcing.shape
    assert n_station == 1
    scale_value = math.sqrt(n_comp * n_station * n_tile * n_point * n_line)
    n_chunk = 4
    phases = reduce_phases(n_line, n_tile)
    n_gram = sum(len(phase_peers(ph, n_line)) for ph in phases)
    n_steps = (n_point - 1).bit_length()
    field = pltpu.VMEM((n_comp, n_cols, n_point), jnp.float32)
    dma = pltpu.SemaphoreType.DMA
    f32 = jnp.float32
    vmem = pl.BlockSpec(memory_space=pltpu.VMEM)
    out = pl.pallas_call(
        functools.partial(kernel, n_line, n_tile, n_chunk, phases, scale_value),
        out_shape=jax.ShapeDtypeStruct((n_comp, n_cols, n_point), f32),
        in_specs=[vmem, vmem, vmem, pl.BlockSpec(memory_space=pltpu.SMEM)],
        out_specs=vmem,
        scratch_shapes=[field] * 7
        + [
            pltpu.VMEM((n_cols, n_point), f32),
            pltpu.VMEM((n_cols, n_point), f32),
            pltpu.VMEM((2, n_cols, n_point), f32),
            pltpu.VMEM((2, n_line - 1, n_cols, n_point), f32),
            pltpu.VMEM((n_cols, n_point), f32),
            pltpu.VMEM((2, ROWS, n_point), f32),
            pltpu.VMEM((n_line - 1, 2, ROWS, n_point), f32),
            pltpu.VMEM((2, n_steps, n_comp, 1, n_point), f32),
            pltpu.VMEM((2, n_comp, 1, n_point), f32),
            pltpu.VMEM((len(phases), n_cols // 2, 2 * n_cols), f32),
            pltpu.VMEM((n_gram, n_cols // 2, 2 * n_cols), f32),
            dma((2, n_chunk, 2)),
            dma((2, n_chunk, 2)),
            dma((n_chunk,)),
            dma((n_chunk,)),
            dma((2, n_chunk, n_line - 1)),
            dma((2, n_chunk, n_line - 1)),
            dma((n_line - 1,)),
            dma((n_line - 1,)),
            dma((n_gram,)),
            dma((n_gram,)),
        ],
        compiler_params=pltpu.CompilerParams(
            collective_id=0, has_side_effects=True, vmem_limit_bytes=32 * 1024 * 1024
        ),
    )(forcing.reshape(n_comp, n_cols, n_point), block_inverse, wall_rates, span_couple)
    return out.reshape(n_comp, n_cols, 1, n_point)


def solution(mesh):
    in_specs = (
        P(None, None, "tile", "line"),
        P(None, None, "tile", "line"),
        P(None, None, "tile", "line"),
        P(),
    )
    out_specs = P(None, None, "tile", "line")
    return jax.shard_map(
        functools.partial(local, mesh.shape["line"], mesh.shape["tile"]),
        mesh=mesh, in_specs=in_specs, out_specs=out_specs, check_vma=False,
    )
```

```python
import functools
import math

import jax
import jax.numpy as jnp
from jax import lax
from jax.experimental import pallas as pl
from jax.experimental.pallas import tpu as pltpu
from jax.sharding import PartitionSpec as P

MESH = pl.DeviceIdType.MESH
ROWS = 8


def reduce_phases(n_line, n_tile):
    pair = 2 if n_tile % 2 == 0 else 1
    phases = [(1, pair, True)]
    stride, rest = pair, n_tile // pair
    while rest > 1:
        factor = 4 if rest % 4 == 0 else next(f for f in range(2, rest + 1) if rest % f == 0)
        phases.append((stride, factor, False))
        stride, rest = stride * factor, rest // factor
    return phases


def phase_peers(phase, n_line):
    stride, factor, with_line = phase
    lines = n_line if with_line else 1
    return [(a, b) for a in range(lines) for b in range(factor) if (a, b) != (0, 0)]


def peer_id(phase, step, n_line):
    stride, factor, _ = phase
    line, tile = lax.axis_index("line"), lax.axis_index("tile")
    digit = lax.rem(lax.div(tile, stride), factor)
    there = lax.rem(digit + step[1], factor)
    return (lax.rem(line + step[0], n_line), tile + (there - digit) * stride)


def scan_strides(n_point):
    strides, by = [], 1
    while by < n_point:
        reach = min(4, -(-n_point // by))
        strides.append((by, reach))
        by *= reach
    return strides


def split(value):
    high = value.astype(jnp.bfloat16)
    low = (value - high.astype(jnp.float32)).astype(jnp.bfloat16)
    return high, low


def eliminate(gram):
    n = gram.shape[0]
    row = lax.broadcasted_iota(jnp.int32, (n, n), 0)
    col = lax.broadcasted_iota(jnp.int32, (n, n), 1)
    both = jnp.concatenate([gram, (row == col).astype(jnp.float32)], axis=1)
    blocks = [both[v * ROWS : (v + 1) * ROWS] for v in range(n // ROWS)]
    shape = (ROWS, 2 * n)
    sub = lax.broadcasted_iota(jnp.int32, shape, 0)
    scales = []
    for q in range(n // ROWS):
        live = range(q, n // ROWS)
        cols = [
            {v: jnp.broadcast_to(blocks[v][:, ROWS * q + c : ROWS * q + c + 1], shape) for v in live}
            for c in range(ROWS)
        ]
        scale = jnp.zeros(shape, jnp.float32)
        for c in range(ROWS):
            pivot = jnp.broadcast_to(cols[c][q][c : c + 1], shape)
            inv = 1.0 / pivot
            scale = jnp.where(sub == c, lax.rsqrt(pivot), scale)
            factor = {v: cols[c][v] * inv for v in live}
            factor[q] = jnp.where(sub > c, factor[q], 0.0)
            top = jnp.broadcast_to(blocks[q][c : c + 1], shape)
            tops = [jnp.broadcast_to(cols[e][q][c : c + 1], shape) for e in range(c + 1, ROWS)]
            for v in live:
                blocks[v] = blocks[v] - factor[v] * top
                for e in range(c + 1, ROWS):
                    cols[e][v] = cols[e][v] - factor[v] * tops[e - c - 1]
        scales.append(scale)
    return jnp.concatenate([b * s for b, s in zip(blocks, scales)], axis=0)[:, n:]


def kernel(
    n_line, n_tile, n_chunk, phases, scale_value,
    f_in, a_in, w_in, s_in, o_out,
    f_ref, a_ref, w_ref, s_ref, o_ref, load_sem, save_sem,
    start, z_low, z_high, rise, y_low, y_high, fall,
    edge_out, edge_in, ends_out, ends_in, enter, rates_out, rates_in, steps, whole,
    gram_out, gram_in, halo_send, halo_recv, edge_send, edge_recv, ends_send, ends_recv,
    rates_send, rates_recv, gram_send, gram_recv,
):
    loads = [
        pltpu.make_async_copy(src, dst, load_sem.at[i])
        for i, (src, dst) in enumerate(
            ((f_in, f_ref), (a_in, a_ref), (w_in, w_ref), (s_in, s_ref))
        )
    ]
    for load in loads:
        load.start()
    n_comp, n_cols, n_point = f_ref.shape
    wide = n_cols // n_chunk
    line, tile = lax.axis_index("line"), lax.axis_index("tile")
    above, below = lax.rem(tile + 1, n_tile), lax.rem(tile + n_tile - 1, n_tile)
    line_peers = [(lax.rem(line + d, n_line), tile) for d in range(1, n_line)]
    lower_line = (lax.rem(line + n_line - 1, n_line), tile)
    gram_peers = [[peer_id(ph, step, n_line) for step in phase_peers(ph, n_line)] for ph in phases]

    greet = [(line, above), (line, below)] + [p for peers in gram_peers for p in peers]
    barrier = pltpu.get_barrier_semaphore()
    for peer in greet:
        pl.semaphore_signal(barrier, inc=1, device_id=peer, device_id_type=MESH)

    started = []

    def send(src, dst, send_sem, recv_sem, peer):
        copy = pltpu.make_async_remote_copy(
            src_ref=src, dst_ref=dst, send_sem=send_sem, recv_sem=recv_sem,
            device_id=peer, device_id_type=MESH,
        )
        copy.start()
        started.append(copy)
        return copy

    def cut(c):
        return pl.ds(c * wide, wide)

    lane3 = lax.broadcasted_iota(jnp.int32, (n_comp, 1, n_point), 2)
    lane = lax.broadcasted_iota(jnp.int32, (wide, n_point), 1)
    lane8 = lax.broadcasted_iota(jnp.int32, (ROWS, n_point), 1)
    lane_big = lax.broadcasted_iota(jnp.int32, (n_comp, wide, n_point), 2)
    strides = scan_strides(n_point)

    def turn(value, by):
        flat = value.reshape(-1, n_point)
        return pltpu.roll(flat, by % n_point, 1).reshape(value.shape)

    def apply_block(value):
        total = a_ref[:, 0] * value[0][None]
        for m in range(1, n_comp):
            total = total + a_ref[:, m] * value[m][None]
        return total

    def pack(value, at):
        packed = jnp.zeros((value.shape[1], n_point), jnp.float32)
        places = lax.broadcasted_iota(jnp.int32, packed.shape, 1)
        for k in range(n_comp):
            packed = jnp.where(places == k, value[k][:, at : at + 1], packed)
        return packed

    def spread(packed):
        return jnp.stack(
            [jnp.broadcast_to(packed[:, k : k + 1], (wide, n_point)) for k in range(n_comp)], axis=0
        )

    def sweep(value, side):
        slot = 0
        for by, reach in strides:
            parts = [turn(value, -by * m if side else by * m) for m in range(1, reach)]
            for part in parts:
                value = value + steps[side, slot] * part
                slot += 1
        return value

    halos = {}
    edges, ends, rates = [], {}, []

    def send_halo(which, c, field, low, high):
        halos[which, c] = [
            send(field.at[:, cut(c)], low.at[:, cut(c)], halo_send.at[which, c, 0],
                 halo_recv.at[which, c, 0], (line, above)),
            send(field.at[:, cut(c)], high.at[:, cut(c)], halo_send.at[which, c, 1],
                 halo_recv.at[which, c, 1], (line, below)),
        ]

    def send_ends(which, c):
        ends[which, c] = [
            send(ends_out.at[which, cut(c)], ends_in.at[which, d, cut(c)], ends_send.at[which, c, d],
                 ends_recv.at[which, c, d], peer)
            for d, peer in enumerate(line_peers)
        ]

    for load in loads:
        load.wait()
    for c in range(n_chunk):
        field = apply_block(f_ref[:, c * wide : (c + 1) * wide])
        start[:, cut(c)] = field
        edge_out[cut(c)] = pack(field, 0)
        if c == 0:
            pl.semaphore_wait(barrier, len(greet))
        send_halo(0, c, start, z_low, z_high)
        edges.append(
            send(edge_out.at[cut(c)], edge_in.at[cut(c)], edge_send.at[c], edge_recv.at[c], lower_line)
        )

    for side in range(2):
        rate = w_ref[side]
        slot = 0
        for by, reach in strides:
            parts = [rate]
            for m in range(1, reach):
                inside = lane3 < n_point - by * m if side else lane3 >= by * m
                steps[side, slot] = jnp.where(inside, rate, 0.0)
                slot += 1
                rate = rate * jnp.where(inside, turn(parts[0], -by * m if side else by * m), 1.0)
        whole[side] = rate
        at = 0 if side else n_point - 1
        total = jnp.zeros((ROWS, n_point), jnp.float32)
        for k in range(n_comp):
            total = jnp.where(lane8 == k, rate[k][:, at : at + 1], total)
        rates_out[side] = total
    for d, peer in enumerate(line_peers):
        rates.append(send(rates_out, rates_in.at[d], rates_send.at[d], rates_recv.at[d], peer))

    def coupled(c, low, high):
        beside = low[:, c * wide : (c + 1) * wide] + high[:, c * wide : (c + 1) * wide]
        return jnp.stack(
            [f_ref[k, c * wide : (c + 1) * wide] + s_ref[k] * beside[k] for k in range(n_comp)], axis=0
        )

    def entry(which, c):
        for copy in ends[which, c]:
            copy.wait_recv()
        total = jnp.zeros((wide, n_point), jnp.float32)
        carried = jnp.ones((1, n_point), jnp.float32)
        for d in range(1, n_line):
            slot = n_line - d - 1 if which else d - 1
            reached = (line + d < n_line) if which else (line >= d)
            reached = reached.astype(jnp.float32)
            total = total + (carried * reached) * ends_in[which, slot, cut(c)]
            carried = carried * rates_in[slot, which, 0:1]
        return total

    def first(c):
        for copy in halos[0, c] + [edges[c]]:
            copy.wait_recv()
        source = apply_block(coupled(c, z_low, z_high))
        last = (line < n_line - 1).astype(jnp.float32)
        over = jnp.where(
            lane_big == n_point - 1, spread(edge_in[cut(c)] * last),
            turn(start[:, c * wide : (c + 1) * wide], -1),
        )
        value = sweep(source + w_ref[1] * over, 0)
        rise[:, cut(c)] = value
        ends_out[0, cut(c)] = pack(value, n_point - 1)
        send_ends(0, c)

    def first_entry(c):
        if c == 0:
            for copy in rates:
                copy.wait_recv()
        total = entry(0, c)
        enter[cut(c)] = total
        rise[:, cut(c)] = rise[:, cut(c)] + whole[0] * spread(total)
        send_halo(1, c, rise, y_low, y_high)

    def second(c):
        for copy in halos[1, c]:
            copy.wait_recv()
        source = apply_block(coupled(c, y_low, y_high))
        under = jnp.where(
            lane_big == 0, spread(enter[cut(c)]), turn(rise[:, c * wide : (c + 1) * wide], 1)
        )
        value = sweep(source + w_ref[0] * under, 1)
        fall[:, cut(c)] = value
        ends_out[1, cut(c)] = pack(value, 0)
        send_ends(1, c)

    def second_entry(c):
        fall[:, cut(c)] = fall[:, cut(c)] + whole[1] * spread(entry(1, c))

    for work, finish in ((first, first_entry), (second, second_entry)):
        for c in range(n_chunk):
            work(c)
            if c:
                finish(c - 1)
        finish(n_chunk - 1)

    total = jnp.zeros((2 * n_cols, 2 * n_cols), jnp.float32)
    for k in range(n_comp):
        both = jnp.concatenate(split(fall[k]), axis=0)
        total = total + lax.dot_general(
            both, both, (((1,), (1,)), ((), ())), preferred_element_type=jnp.float32
        )
    gram = total[:n_cols] + total[n_cols:]
    gram = gram[:, :n_cols] + gram[:, n_cols:]
    half = n_cols // 2
    packed = jnp.concatenate([gram[:half], gram[half:]], axis=1)
    slot = 0
    for i, peers in enumerate(gram_peers):
        gram_out[i] = packed
        copies = []
        for peer in peers:
            copies.append(
                send(gram_out.at[i], gram_in.at[slot], gram_send.at[slot], gram_recv.at[slot], peer)
            )
            slot += 1
        for j, copy in enumerate(copies):
            copy.wait_recv()
            packed = packed + gram_in[slot - len(copies) + j]
    gram = jnp.concatenate([packed[:, :n_cols], packed[:, n_cols:]], axis=0)

    high, low = split(eliminate(gram) * scale_value)
    left = jnp.concatenate([high, high, low], axis=1)
    saves = []
    for k in range(n_comp):
        top, rest = split(fall[k])
        o_ref[k] = jnp.dot(
            left, jnp.concatenate([top, rest, top], axis=0), preferred_element_type=jnp.float32
        )
        saves.append(pltpu.make_async_copy(o_ref.at[k], o_out.at[k], save_sem.at[k]))
        saves[k].start()
    for save in saves:
        save.wait()
    for copy in started:
        copy.wait_send()


def local(n_line, n_tile, forcing, block_inverse, wall_rates, span_couple):
    n_comp, n_cols, n_station, n_point = forcing.shape
    assert n_station == 1
    scale_value = math.sqrt(n_comp * n_station * n_tile * n_point * n_line)
    n_chunk = 4
    phases = reduce_phases(n_line, n_tile)
    n_gram = sum(len(phase_peers(ph, n_line)) for ph in phases)
    n_steps = sum(reach - 1 for _, reach in scan_strides(n_point))
    field = pltpu.VMEM((n_comp, n_cols, n_point), jnp.float32)
    dma = pltpu.SemaphoreType.DMA
    f32 = jnp.float32
    out = pl.pallas_call(
        functools.partial(kernel, n_line, n_tile, n_chunk, phases, scale_value),
        out_shape=jax.ShapeDtypeStruct((n_comp, n_cols, n_point), f32),
        in_specs=[pl.BlockSpec(memory_space=pltpu.HBM)] * 4,
        out_specs=pl.BlockSpec(memory_space=pltpu.HBM),
        scratch_shapes=[
            field,
            pltpu.VMEM(block_inverse.shape, f32),
            pltpu.VMEM(wall_rates.shape, f32),
            pltpu.SMEM(span_couple.shape, f32),
            field,
            dma((4,)),
            dma((n_comp,)),
        ]
        + [field] * 7
        + [
            pltpu.VMEM((n_cols, n_point), f32),
            pltpu.VMEM((n_cols, n_point), f32),
            pltpu.VMEM((2, n_cols, n_point), f32),
            pltpu.VMEM((2, n_line - 1, n_cols, n_point), f32),
            pltpu.VMEM((n_cols, n_point), f32),
            pltpu.VMEM((2, ROWS, n_point), f32),
            pltpu.VMEM((n_line - 1, 2, ROWS, n_point), f32),
            pltpu.VMEM((2, n_steps, n_comp, 1, n_point), f32),
            pltpu.VMEM((2, n_comp, 1, n_point), f32),
            pltpu.VMEM((len(phases), n_cols // 2, 2 * n_cols), f32),
            pltpu.VMEM((n_gram, n_cols // 2, 2 * n_cols), f32),
            dma((2, n_chunk, 2)),
            dma((2, n_chunk, 2)),
            dma((n_chunk,)),
            dma((n_chunk,)),
            dma((2, n_chunk, n_line - 1)),
            dma((2, n_chunk, n_line - 1)),
            dma((n_line - 1,)),
            dma((n_line - 1,)),
            dma((n_gram,)),
            dma((n_gram,)),
        ],
        compiler_params=pltpu.CompilerParams(
            collective_id=0, has_side_effects=True, vmem_limit_bytes=64 * 1024 * 1024
        ),
    )(forcing.reshape(n_comp, n_cols, n_point), block_inverse, wall_rates, span_couple)
    return out.reshape(n_comp, n_cols, 1, n_point)


def solution(mesh):
    in_specs = (
        P(None, None, "tile", "line"),
        P(None, None, "tile", "line"),
        P(None, None, "tile", "line"),
        P(),
    )
    out_specs = P(None, None, "tile", "line")
    return jax.shard_map(
        functools.partial(local, mesh.shape["line"], mesh.shape["tile"]),
        mesh=mesh, in_specs=in_specs, out_specs=out_specs, check_vma=False,
    )
```

```python
import functools
import math

import jax
import jax.numpy as jnp
from jax import lax
from jax.experimental import pallas as pl
from jax.experimental.pallas import tpu as pltpu
from jax.sharding import PartitionSpec as P

MESH = pl.DeviceIdType.MESH
ROWS = 8


def reduce_phases(n_line, n_tile):
    pair = 2 if n_tile % 2 == 0 else 1
    phases = [(1, pair, True)]
    stride, rest = pair, n_tile // pair
    while rest > 1:
        factor = 4 if rest % 4 == 0 else next(f for f in range(2, rest + 1) if rest % f == 0)
        phases.append((stride, factor, False))
        stride, rest = stride * factor, rest // factor
    return phases


def phase_peers(phase, n_line):
    stride, factor, with_line = phase
    lines = n_line if with_line else 1
    return [(a, b) for a in range(lines) for b in range(factor) if (a, b) != (0, 0)]


def peer_id(phase, step, n_line):
    stride, factor, _ = phase
    line, tile = lax.axis_index("line"), lax.axis_index("tile")
    digit = lax.rem(lax.div(tile, stride), factor)
    there = lax.rem(digit + step[1], factor)
    return (lax.rem(line + step[0], n_line), tile + (there - digit) * stride)


def scan_strides(n_point):
    strides, by = [], 1
    while by < n_point:
        reach = min(4, -(-n_point // by))
        strides.append((by, reach))
        by *= reach
    return strides


def split(value):
    high = value.astype(jnp.bfloat16)
    low = (value - high.astype(jnp.float32)).astype(jnp.bfloat16)
    return high, low


def eliminate(square, right):
    n, shape = square.shape[0], (ROWS, right.shape[1])
    groups = n // ROWS
    sub = lax.broadcasted_iota(jnp.int32, shape, 0)
    blocks = [right[v * ROWS : (v + 1) * ROWS] for v in range(groups)]
    cols = [
        [jnp.broadcast_to(square[v * ROWS : (v + 1) * ROWS, e : e + 1], shape) for v in range(groups)]
        for e in range(n)
    ]
    scales = [jnp.zeros(shape, jnp.float32)] * groups
    for p in range(n):
        q, c = divmod(p, ROWS)
        pivot = jnp.broadcast_to(cols[p][q][c : c + 1], shape)
        inv = 1.0 / pivot
        scales[q] = jnp.where(sub == c, lax.rsqrt(pivot), scales[q])
        top = jnp.broadcast_to(blocks[q][c : c + 1], shape)
        tops = {e: jnp.broadcast_to(cols[e][q][c : c + 1], shape) for e in range(p + 1, n)}
        for v in range(q, groups):
            factor = cols[p][v] * inv
            if v == q:
                factor = jnp.where(sub > c, factor, 0.0)
            blocks[v] = blocks[v] - factor * top
            for e in range(p + 1, n):
                cols[e][v] = cols[e][v] - factor * tops[e]
    return jnp.concatenate([b * t for b, t in zip(blocks, scales)], axis=0)


def kernel(
    n_line, n_tile, n_chunk, phases, scale_value,
    f_in, a_in, w_in, s_in, o_ref,
    f_ref, a_ref, w_ref, s_ref, load_sem,
    start, z_low, z_high, rise, y_low, y_high, fall,
    edge_out, edge_in, ends_out, ends_in, enter, rates_out, rates_in, steps, whole,
    high, low, gram_out, gram_in, halo_send, halo_recv, edge_send, edge_recv, ends_send, ends_recv,
    rates_send, rates_recv, gram_send, gram_recv,
):
    loads = [
        pltpu.make_async_copy(src, dst, load_sem.at[i])
        for i, (src, dst) in enumerate(
            ((f_in, f_ref), (a_in, a_ref), (w_in, w_ref), (s_in, s_ref))
        )
    ]
    for load in loads:
        load.start()
    n_comp, n_cols, n_point = f_ref.shape
    wide = n_cols // n_chunk
    line, tile = lax.axis_index("line"), lax.axis_index("tile")
    above, below = lax.rem(tile + 1, n_tile), lax.rem(tile + n_tile - 1, n_tile)
    line_peers = [(lax.rem(line + d, n_line), tile) for d in range(1, n_line)]
    lower_line = (lax.rem(line + n_line - 1, n_line), tile)
    gram_peers = [[peer_id(ph, step, n_line) for step in phase_peers(ph, n_line)] for ph in phases]

    greet = [(line, above), (line, below)] + [p for peers in gram_peers for p in peers]
    barrier = pltpu.get_barrier_semaphore()
    for peer in greet:
        pl.semaphore_signal(barrier, inc=1, device_id=peer, device_id_type=MESH)

    started = []

    def send(src, dst, send_sem, recv_sem, peer):
        copy = pltpu.make_async_remote_copy(
            src_ref=src, dst_ref=dst, send_sem=send_sem, recv_sem=recv_sem,
            device_id=peer, device_id_type=MESH,
        )
        copy.start()
        started.append(copy)
        return copy

    def cut(c):
        return pl.ds(c * wide, wide)

    lane3 = lax.broadcasted_iota(jnp.int32, (n_comp, 1, n_point), 2)
    lane = lax.broadcasted_iota(jnp.int32, (wide, n_point), 1)
    lane8 = lax.broadcasted_iota(jnp.int32, (ROWS, n_point), 1)
    lane_big = lax.broadcasted_iota(jnp.int32, (n_comp, wide, n_point), 2)
    strides = scan_strides(n_point)

    def turn(value, by):
        flat = value.reshape(-1, n_point)
        return pltpu.roll(flat, by % n_point, 1).reshape(value.shape)

    def apply_block(value):
        total = a_ref[:, 0] * value[0][None]
        for m in range(1, n_comp):
            total = total + a_ref[:, m] * value[m][None]
        return total

    def pack(value, at):
        packed = jnp.zeros((value.shape[1], n_point), jnp.float32)
        places = lax.broadcasted_iota(jnp.int32, packed.shape, 1)
        for k in range(n_comp):
            packed = jnp.where(places == k, value[k][:, at : at + 1], packed)
        return packed

    def spread(packed):
        return jnp.stack(
            [jnp.broadcast_to(packed[:, k : k + 1], (wide, n_point)) for k in range(n_comp)], axis=0
        )

    def sweep(value, side):
        slot = 0
        for by, reach in strides:
            parts = [turn(value, -by * m if side else by * m) for m in range(1, reach)]
            for part in parts:
                value = value + steps[side, slot] * part
                slot += 1
        return value

    halos = {}
    edges, ends, rates = [], {}, []

    def send_halo(which, c, field, low, high):
        halos[which, c] = [
            send(field.at[:, cut(c)], low.at[:, cut(c)], halo_send.at[which, c, 0],
                 halo_recv.at[which, c, 0], (line, above)),
            send(field.at[:, cut(c)], high.at[:, cut(c)], halo_send.at[which, c, 1],
                 halo_recv.at[which, c, 1], (line, below)),
        ]

    def send_ends(which, c):
        ends[which, c] = [
            send(ends_out.at[which, cut(c)], ends_in.at[which, d, cut(c)], ends_send.at[which, c, d],
                 ends_recv.at[which, c, d], peer)
            for d, peer in enumerate(line_peers)
        ]

    for load in loads:
        load.wait()
    for c in range(n_chunk):
        field = apply_block(f_ref[:, c * wide : (c + 1) * wide])
        start[:, cut(c)] = field
        edge_out[cut(c)] = pack(field, 0)
        if c == 0:
            pl.semaphore_wait(barrier, len(greet))
        send_halo(0, c, start, z_low, z_high)
        edges.append(
            send(edge_out.at[cut(c)], edge_in.at[cut(c)], edge_send.at[c], edge_recv.at[c], lower_line)
        )

    for side in range(2):
        rate = w_ref[side]
        slot = 0
        for by, reach in strides:
            parts = [rate]
            for m in range(1, reach):
                inside = lane3 < n_point - by * m if side else lane3 >= by * m
                steps[side, slot] = jnp.where(inside, rate, 0.0)
                slot += 1
                rate = rate * jnp.where(inside, turn(parts[0], -by * m if side else by * m), 1.0)
        whole[side] = rate
        at = 0 if side else n_point - 1
        total = jnp.zeros((ROWS, n_point), jnp.float32)
        for k in range(n_comp):
            total = jnp.where(lane8 == k, rate[k][:, at : at + 1], total)
        rates_out[side] = total
    for d, peer in enumerate(line_peers):
        rates.append(send(rates_out, rates_in.at[d], rates_send.at[d], rates_recv.at[d], peer))

    def coupled(c, low, high):
        beside = low[:, c * wide : (c + 1) * wide] + high[:, c * wide : (c + 1) * wide]
        return jnp.stack(
            [f_ref[k, c * wide : (c + 1) * wide] + s_ref[k] * beside[k] for k in range(n_comp)], axis=0
        )

    def entry(which, c):
        for copy in ends[which, c]:
            copy.wait_recv()
        total = jnp.zeros((wide, n_point), jnp.float32)
        carried = jnp.ones((1, n_point), jnp.float32)
        for d in range(1, n_line):
            slot = n_line - d - 1 if which else d - 1
            reached = (line + d < n_line) if which else (line >= d)
            reached = reached.astype(jnp.float32)
            total = total + (carried * reached) * ends_in[which, slot, cut(c)]
            carried = carried * rates_in[slot, which, 0:1]
        return total

    def first(c):
        for copy in halos[0, c] + [edges[c]]:
            copy.wait_recv()
        source = apply_block(coupled(c, z_low, z_high))
        last = (line < n_line - 1).astype(jnp.float32)
        over = jnp.where(
            lane_big == n_point - 1, spread(edge_in[cut(c)] * last),
            turn(start[:, c * wide : (c + 1) * wide], -1),
        )
        value = sweep(source + w_ref[1] * over, 0)
        rise[:, cut(c)] = value
        ends_out[0, cut(c)] = pack(value, n_point - 1)
        send_ends(0, c)

    def first_entry(c):
        if c == 0:
            for copy in rates:
                copy.wait_recv()
        total = entry(0, c)
        enter[cut(c)] = total
        rise[:, cut(c)] = rise[:, cut(c)] + whole[0] * spread(total)
        send_halo(1, c, rise, y_low, y_high)

    def second(c):
        for copy in halos[1, c]:
            copy.wait_recv()
        source = apply_block(coupled(c, y_low, y_high))
        under = jnp.where(
            lane_big == 0, spread(enter[cut(c)]), turn(rise[:, c * wide : (c + 1) * wide], 1)
        )
        value = sweep(source + w_ref[0] * under, 1)
        fall[:, cut(c)] = value
        ends_out[1, cut(c)] = pack(value, 0)
        send_ends(1, c)

    def second_entry(c):
        fall[:, cut(c)] = fall[:, cut(c)] + whole[1] * spread(entry(1, c))

    def panel(c):
        till = (c + 1) * wide
        parts = [split(fall[k, cut(c)]) for k in range(n_comp)]
        for k, (top, rest) in enumerate(parts):
            high[k, cut(c)], low[k, cut(c)] = top, rest
        tops = jnp.concatenate([top for top, _ in parts], axis=1)
        left = jnp.concatenate([tops, jnp.concatenate([rest for _, rest in parts], axis=1)], axis=0)
        both = lax.dot_general(
            left, jnp.concatenate([high[k, :till] for k in range(n_comp)], axis=1),
            (((1,), (1,)), ((), ())), preferred_element_type=jnp.float32,
        )
        cross = lax.dot_general(
            tops, jnp.concatenate([low[k, :till] for k in range(n_comp)], axis=1),
            (((1,), (1,)), ((), ())), preferred_element_type=jnp.float32,
        )
        rows = both[:wide] + both[wide:] + cross
        if till < n_cols:
            rows = jnp.concatenate([rows, jnp.zeros((wide, n_cols - till), jnp.float32)], axis=1)
        return jnp.concatenate([rows[: wide // 2], rows[wide // 2 :]], axis=1)

    sums, flights, factor_rows = {}, {}, []

    def gram_send_phase(c, i):
        gram_out[c, i] = sums[c]
        slot = sum(len(peers) for peers in gram_peers[:i])
        flights[c] = []
        for j, peer in enumerate(gram_peers[i]):
            at = slot + j
            copy = send(gram_out.at[c, i], gram_in.at[c, at], gram_send.at[c, at],
                        gram_recv.at[c, at], peer)
            flights[c].append((copy, at))

    def gram_collect(c):
        for copy, at in flights[c]:
            copy.wait_recv()
            sums[c] = sums[c] + gram_in[c, at]

    def dot(left, right, transposed):
        return lax.dot_general(
            left, right, (((1,), (1 if transposed else 0,)), ((), ())),
            precision=lax.Precision.HIGHEST, preferred_element_type=jnp.float32,
        )

    def factor(c):
        from_col, till = c * wide, (c + 1) * wide
        rows = jnp.concatenate([sums[c][:, :n_cols], sums[c][:, n_cols:]], axis=0)
        square = rows[:, from_col:till]
        row = lax.broadcasted_iota(jnp.int32, (wide, n_cols), 0)
        col = lax.broadcasted_iota(jnp.int32, (wide, n_cols), 1)
        right = (col == row + from_col).astype(jnp.float32)
        if c:
            known = jnp.concatenate(factor_rows, axis=0)
            lower = dot(rows, known, True)
            square = square - dot(lower, lower, True)
            right = right - dot(lower, known, False)
        factor_rows.append(eliminate(square, right))
        top, rest = split(factor_rows[c][:, :till] * scale_value)
        left = jnp.concatenate([top, rest], axis=0)
        for k in range(n_comp):
            both = jnp.dot(left, high[k, :till], preferred_element_type=jnp.float32)
            cross = jnp.dot(top, low[k, :till], preferred_element_type=jnp.float32)
            o_ref[k, cut(c)] = both[:wide] + both[wide:] + cross

    for c in range(n_chunk):
        first(c)
        if c:
            first_entry(c - 1)
    first_entry(n_chunk - 1)

    def stage(c, which):
        if which == 0:
            second(c)
            return
        if which == 1:
            second_entry(c)
            sums[c] = panel(c)
        else:
            gram_collect(c)
        if which <= len(phases):
            gram_send_phase(c, which - 1)
        else:
            factor(c)

    n_stages = len(phases) + 2
    for now in range(n_chunk + n_stages - 1):
        for c in range(min(now, n_chunk - 1), -1, -1):
            if now - c < n_stages:
                stage(c, now - c)
    for copy in started:
        copy.wait_send()


def local(n_line, n_tile, forcing, block_inverse, wall_rates, span_couple):
    n_comp, n_cols, n_station, n_point = forcing.shape
    assert n_station == 1
    scale_value = math.sqrt(n_comp * n_station * n_tile * n_point * n_line)
    n_chunk = 4
    half = n_cols // n_chunk // 2
    phases = reduce_phases(n_line, n_tile)
    n_gram = sum(len(phase_peers(ph, n_line)) for ph in phases)
    n_steps = sum(reach - 1 for _, reach in scan_strides(n_point))
    field = pltpu.VMEM((n_comp, n_cols, n_point), jnp.float32)
    dma = pltpu.SemaphoreType.DMA
    f32 = jnp.float32
    inputs = (forcing.reshape(n_comp, n_cols, n_point), block_inverse, wall_rates, span_couple)
    out = pl.pallas_call(
        functools.partial(kernel, n_line, n_tile, n_chunk, phases, scale_value),
        out_shape=pltpu.VMEM((n_comp, n_cols, n_point), f32),
        in_specs=[pl.BlockSpec(memory_space=pltpu.HBM)] * 4,
        out_specs=pl.BlockSpec(memory_space=pltpu.VMEM),
        scratch_shapes=[
            field,
            pltpu.VMEM(block_inverse.shape, f32),
            pltpu.VMEM(wall_rates.shape, f32),
            pltpu.SMEM(span_couple.shape, f32),
            dma((4,)),
        ]
        + [field] * 7
        + [
            pltpu.VMEM((n_cols, n_point), f32),
            pltpu.VMEM((n_cols, n_point), f32),
            pltpu.VMEM((2, n_cols, n_point), f32),
            pltpu.VMEM((2, n_line - 1, n_cols, n_point), f32),
            pltpu.VMEM((n_cols, n_point), f32),
            pltpu.VMEM((2, ROWS, n_point), f32),
            pltpu.VMEM((n_line - 1, 2, ROWS, n_point), f32),
            pltpu.VMEM((2, n_steps, n_comp, 1, n_point), f32),
            pltpu.VMEM((2, n_comp, 1, n_point), f32),
            pltpu.VMEM((n_comp, n_cols, n_point), jnp.bfloat16),
            pltpu.VMEM((n_comp, n_cols, n_point), jnp.bfloat16),
            pltpu.VMEM((n_chunk, len(phases), half, 2 * n_cols), f32),
            pltpu.VMEM((n_chunk, n_gram, half, 2 * n_cols), f32),
            dma((2, n_chunk, 2)),
            dma((2, n_chunk, 2)),
            dma((n_chunk,)),
            dma((n_chunk,)),
            dma((2, n_chunk, n_line - 1)),
            dma((2, n_chunk, n_line - 1)),
            dma((n_line - 1,)),
            dma((n_line - 1,)),
            dma((n_chunk, n_gram)),
            dma((n_chunk, n_gram)),
        ],
        compiler_params=pltpu.CompilerParams(
            collective_id=0, has_side_effects=True, vmem_limit_bytes=32 * 1024 * 1024
        ),
    )(*[pltpu.with_memory_space_constraint(value, pltpu.HBM) for value in inputs])
    return out.reshape(n_comp, n_cols, 1, n_point)


def solution(mesh):
    in_specs = (
        P(None, None, "tile", "line"),
        P(None, None, "tile", "line"),
        P(None, None, "tile", "line"),
        P(),
    )
    out_specs = P(None, None, "tile", "line")
    return jax.shard_map(
        functools.partial(local, mesh.shape["line"], mesh.shape["tile"]),
        mesh=mesh, in_specs=in_specs, out_specs=out_specs, check_vma=False,
    )
```

```python
import functools
import math

import jax
import jax.numpy as jnp
from jax import lax
from jax.experimental import pallas as pl
from jax.experimental.pallas import tpu as pltpu
from jax.sharding import PartitionSpec as P

MESH = pl.DeviceIdType.MESH
ROWS = 8


def reduce_phases(n_line, n_tile):
    pair = 2 if n_tile % 2 == 0 else 1
    phases = [(1, pair, True)]
    stride, rest = pair, n_tile // pair
    while rest > 1:
        factor = 4 if rest % 4 == 0 else next(f for f in range(2, rest + 1) if rest % f == 0)
        phases.append((stride, factor, False))
        stride, rest = stride * factor, rest // factor
    return phases


def phase_peers(phase, n_line):
    stride, factor, with_line = phase
    lines = n_line if with_line else 1
    return [(a, b) for a in range(lines) for b in range(factor) if (a, b) != (0, 0)]


def peer_id(phase, step, n_line):
    stride, factor, _ = phase
    line, tile = lax.axis_index("line"), lax.axis_index("tile")
    digit = lax.rem(lax.div(tile, stride), factor)
    there = lax.rem(digit + step[1], factor)
    return (lax.rem(line + step[0], n_line), tile + (there - digit) * stride)


def scan_strides(n_point):
    strides, by = [], 1
    while by < n_point:
        reach = min(4, -(-n_point // by))
        strides.append((by, reach))
        by *= reach
    return strides


def split(value):
    high = value.astype(jnp.bfloat16)
    low = (value - high.astype(jnp.float32)).astype(jnp.bfloat16)
    return high, low


def eliminate(square, right):
    n, shape = square.shape[0], (ROWS, right.shape[1])
    groups = n // ROWS
    sub = lax.broadcasted_iota(jnp.int32, shape, 0)
    blocks = [right[v * ROWS : (v + 1) * ROWS] for v in range(groups)]
    cols = [
        [jnp.broadcast_to(square[v * ROWS : (v + 1) * ROWS, e : e + 1], shape) for v in range(groups)]
        for e in range(n)
    ]
    scales = [jnp.zeros(shape, jnp.float32)] * groups
    for p in range(n):
        q, c = divmod(p, ROWS)
        pivot = jnp.broadcast_to(cols[p][q][c : c + 1], shape)
        inv = 1.0 / pivot
        scales[q] = jnp.where(sub == c, lax.rsqrt(pivot), scales[q])
        top = jnp.broadcast_to(blocks[q][c : c + 1], shape)
        tops = {e: jnp.broadcast_to(cols[e][q][c : c + 1], shape) for e in range(p + 1, n)}
        for v in range(q, groups):
            factor = cols[p][v] * inv
            if v == q:
                factor = jnp.where(sub > c, factor, 0.0)
            blocks[v] = blocks[v] - factor * top
            for e in range(p + 1, n):
                cols[e][v] = cols[e][v] - factor * tops[e]
    return jnp.concatenate([b * t for b, t in zip(blocks, scales)], axis=0)


def kernel(
    n_line, n_tile, n_chunk, phases, scale_value,
    f_in, a_in, w_in, s_in, o_ref,
    f_ref, a_ref, w_ref, s_ref, load_sem,
    start, z_low, z_high, rise, y_low, y_high, fall,
    edge_out, edge_in, ends_out, ends_in, enter, rates_out, rates_in, steps, whole,
    high, low, gram_out, gram_in, halo_send, halo_recv, edge_send, edge_recv, ends_send, ends_recv,
    rates_send, rates_recv, gram_send, gram_recv,
):
    loads = [
        pltpu.make_async_copy(src, dst, load_sem.at[i])
        for i, (src, dst) in enumerate(
            ((f_in, f_ref), (a_in, a_ref), (w_in, w_ref), (s_in, s_ref))
        )
    ]
    for load in loads:
        load.start()
    n_comp, n_cols, n_point = f_ref.shape
    wide = n_cols // n_chunk
    line, tile = lax.axis_index("line"), lax.axis_index("tile")
    above, below = lax.rem(tile + 1, n_tile), lax.rem(tile + n_tile - 1, n_tile)
    line_peers = [(lax.rem(line + d, n_line), tile) for d in range(1, n_line)]
    lower_line = (lax.rem(line + n_line - 1, n_line), tile)
    gram_peers = [[peer_id(ph, step, n_line) for step in phase_peers(ph, n_line)] for ph in phases]

    greet = [(line, above), (line, below)] + [p for peers in gram_peers for p in peers]
    barrier = pltpu.get_barrier_semaphore()
    for peer in greet:
        pl.semaphore_signal(barrier, inc=1, device_id=peer, device_id_type=MESH)

    started = []

    def send(src, dst, send_sem, recv_sem, peer):
        copy = pltpu.make_async_remote_copy(
            src_ref=src, dst_ref=dst, send_sem=send_sem, recv_sem=recv_sem,
            device_id=peer, device_id_type=MESH,
        )
        copy.start()
        started.append(copy)
        return copy

    def cut(c):
        return pl.ds(c * wide, wide)

    lane3 = lax.broadcasted_iota(jnp.int32, (n_comp, 1, n_point), 2)
    lane = lax.broadcasted_iota(jnp.int32, (wide, n_point), 1)
    lane8 = lax.broadcasted_iota(jnp.int32, (ROWS, n_point), 1)
    lane_big = lax.broadcasted_iota(jnp.int32, (n_comp, wide, n_point), 2)
    strides = scan_strides(n_point)

    def turn(value, by):
        flat = value.reshape(-1, n_point)
        return pltpu.roll(flat, by % n_point, 1).reshape(value.shape)

    def apply_block(value):
        total = a_ref[:, 0] * value[0][None]
        for m in range(1, n_comp):
            total = total + a_ref[:, m] * value[m][None]
        return total

    def pack(value, at):
        packed = jnp.zeros((value.shape[1], n_point), jnp.float32)
        places = lax.broadcasted_iota(jnp.int32, packed.shape, 1)
        for k in range(n_comp):
            packed = jnp.where(places == k, value[k][:, at : at + 1], packed)
        return packed

    def spread(packed):
        return jnp.stack(
            [jnp.broadcast_to(packed[:, k : k + 1], (wide, n_point)) for k in range(n_comp)], axis=0
        )

    def sweep(value, side):
        slot = 0
        for by, reach in strides:
            parts = [turn(value, -by * m if side else by * m) for m in range(1, reach)]
            for part in parts:
                value = value + steps[side, slot] * part
                slot += 1
        return value

    halos = {}
    edges, ends, rates = [], {}, []

    def send_halo(which, c, field, low, high):
        halos[which, c] = [
            send(field.at[:, cut(c)], low.at[:, cut(c)], halo_send.at[which, c, 0],
                 halo_recv.at[which, c, 0], (line, above)),
            send(field.at[:, cut(c)], high.at[:, cut(c)], halo_send.at[which, c, 1],
                 halo_recv.at[which, c, 1], (line, below)),
        ]

    def send_ends(which, c):
        ends[which, c] = [
            send(ends_out.at[which, cut(c)], ends_in.at[which, d, cut(c)], ends_send.at[which, c, d],
                 ends_recv.at[which, c, d], peer)
            for d, peer in enumerate(line_peers)
        ]

    for load in loads:
        load.wait()
    for c in range(n_chunk):
        field = apply_block(f_ref[:, c * wide : (c + 1) * wide])
        start[:, cut(c)] = field
        edge_out[cut(c)] = pack(field, 0)
        if c == 0:
            pl.semaphore_wait(barrier, len(greet))
        send_halo(0, c, start, z_low, z_high)
        edges.append(
            send(edge_out.at[cut(c)], edge_in.at[cut(c)], edge_send.at[c], edge_recv.at[c], lower_line)
        )

    for side in range(2):
        rate = w_ref[side]
        slot = 0
        for by, reach in strides:
            parts = [rate]
            for m in range(1, reach):
                inside = lane3 < n_point - by * m if side else lane3 >= by * m
                steps[side, slot] = jnp.where(inside, rate, 0.0)
                slot += 1
                rate = rate * jnp.where(inside, turn(parts[0], -by * m if side else by * m), 1.0)
        whole[side] = rate
        at = 0 if side else n_point - 1
        total = jnp.zeros((ROWS, n_point), jnp.float32)
        for k in range(n_comp):
            total = jnp.where(lane8 == k, rate[k][:, at : at + 1], total)
        rates_out[side] = total
    for d, peer in enumerate(line_peers):
        rates.append(send(rates_out, rates_in.at[d], rates_send.at[d], rates_recv.at[d], peer))

    def coupled(c, low, high):
        beside = low[:, c * wide : (c + 1) * wide] + high[:, c * wide : (c + 1) * wide]
        return jnp.stack(
            [f_ref[k, c * wide : (c + 1) * wide] + s_ref[k] * beside[k] for k in range(n_comp)], axis=0
        )

    def entry(which, c):
        for copy in ends[which, c]:
            copy.wait_recv()
        total = jnp.zeros((wide, n_point), jnp.float32)
        carried = jnp.ones((1, n_point), jnp.float32)
        for d in range(1, n_line):
            slot = n_line - d - 1 if which else d - 1
            reached = (line + d < n_line) if which else (line >= d)
            reached = reached.astype(jnp.float32)
            total = total + (carried * reached) * ends_in[which, slot, cut(c)]
            carried = carried * rates_in[slot, which, 0:1]
        return total

    def first(c):
        for copy in halos[0, c] + [edges[c]]:
            copy.wait_recv()
        source = apply_block(coupled(c, z_low, z_high))
        last = (line < n_line - 1).astype(jnp.float32)
        over = jnp.where(
            lane_big == n_point - 1, spread(edge_in[cut(c)] * last),
            turn(start[:, c * wide : (c + 1) * wide], -1),
        )
        value = sweep(source + w_ref[1] * over, 0)
        rise[:, cut(c)] = value
        ends_out[0, cut(c)] = pack(value, n_point - 1)
        send_ends(0, c)

    def first_entry(c):
        if c == 0:
            for copy in rates:
                copy.wait_recv()
        total = entry(0, c)
        enter[cut(c)] = total
        rise[:, cut(c)] = rise[:, cut(c)] + whole[0] * spread(total)
        send_halo(1, c, rise, y_low, y_high)

    def second(c):
        for copy in halos[1, c]:
            copy.wait_recv()
        source = apply_block(coupled(c, y_low, y_high))
        under = jnp.where(
            lane_big == 0, spread(enter[cut(c)]), turn(rise[:, c * wide : (c + 1) * wide], 1)
        )
        value = sweep(source + w_ref[0] * under, 1)
        fall[:, cut(c)] = value
        ends_out[1, cut(c)] = pack(value, 0)
        send_ends(1, c)

    def second_entry(c):
        fall[:, cut(c)] = fall[:, cut(c)] + whole[1] * spread(entry(1, c))

    def panel(c):
        till = (c + 1) * wide
        parts = [split(fall[k, cut(c)]) for k in range(n_comp)]
        for k, (top, rest) in enumerate(parts):
            high[k, cut(c)], low[k, cut(c)] = top, rest
        tops = jnp.concatenate([top for top, _ in parts], axis=1)
        left = jnp.concatenate([tops, jnp.concatenate([rest for _, rest in parts], axis=1)], axis=0)
        both = lax.dot_general(
            left, jnp.concatenate([high[k, :till] for k in range(n_comp)], axis=1),
            (((1,), (1,)), ((), ())), preferred_element_type=jnp.float32,
        )
        cross = lax.dot_general(
            tops, jnp.concatenate([low[k, :till] for k in range(n_comp)], axis=1),
            (((1,), (1,)), ((), ())), preferred_element_type=jnp.float32,
        )
        rows = both[:wide] + both[wide:] + cross
        if till < n_cols:
            rows = jnp.concatenate([rows, jnp.zeros((wide, n_cols - till), jnp.float32)], axis=1)
        return jnp.concatenate([rows[: wide // 2], rows[wide // 2 :]], axis=1)

    sums, flights, factor_rows = {}, {}, []

    def gram_send_phase(c, i):
        gram_out[c, i] = sums[c]
        slot = sum(len(peers) for peers in gram_peers[:i])
        flights[c] = []
        for j, peer in enumerate(gram_peers[i]):
            at = slot + j
            copy = send(gram_out.at[c, i], gram_in.at[c, at], gram_send.at[c, at],
                        gram_recv.at[c, at], peer)
            flights[c].append((copy, at))

    def gram_collect(c):
        for copy, at in flights[c]:
            copy.wait_recv()
            sums[c] = sums[c] + gram_in[c, at]

    def dot(left, right, transposed):
        return lax.dot_general(
            left, right, (((1,), (1 if transposed else 0,)), ((), ())),
            precision=lax.Precision.HIGHEST, preferred_element_type=jnp.float32,
        )

    def factor(c):
        from_col, till = c * wide, (c + 1) * wide
        rows = jnp.concatenate([sums[c][:, :n_cols], sums[c][:, n_cols:]], axis=0)
        square = rows[:, from_col:till]
        row = lax.broadcasted_iota(jnp.int32, (wide, n_cols), 0)
        col = lax.broadcasted_iota(jnp.int32, (wide, n_cols), 1)
        right = (col == row + from_col).astype(jnp.float32)
        if c:
            known = jnp.concatenate(factor_rows, axis=0)
            lower = dot(rows, known, True)
            square = square - dot(lower, lower, True)
            right = right - dot(lower, known, False)
        factor_rows.append(eliminate(square, right))
        top, rest = split(factor_rows[c][:, :till] * scale_value)
        left = jnp.concatenate([top, rest], axis=0)
        for k in range(n_comp):
            both = jnp.dot(left, high[k, :till], preferred_element_type=jnp.float32)
            cross = jnp.dot(top, low[k, :till], preferred_element_type=jnp.float32)
            o_ref[k, cut(c)] = both[:wide] + both[wide:] + cross

    for c in range(n_chunk):
        first(c)
        if c:
            first_entry(c - 1)
    first_entry(n_chunk - 1)

    def stage(c, which):
        if which == 0:
            second(c)
            return
        if which == 1:
            second_entry(c)
            sums[c] = panel(c)
        else:
            gram_collect(c)
        if which <= len(phases):
            gram_send_phase(c, which - 1)
        else:
            factor(c)

    n_stages = len(phases) + 2
    for now in range(n_chunk + n_stages - 1):
        for c in range(min(now, n_chunk - 1), -1, -1):
            if now - c < n_stages:
                stage(c, now - c)
    for copy in started:
        copy.wait_send()


def local(n_line, n_tile, forcing, block_inverse, wall_rates, span_couple):
    n_comp, n_cols, n_station, n_point = forcing.shape
    assert n_station == 1
    scale_value = math.sqrt(n_comp * n_station * n_tile * n_point * n_line)
    n_chunk = 2
    half = n_cols // n_chunk // 2
    phases = reduce_phases(n_line, n_tile)
    n_gram = sum(len(phase_peers(ph, n_line)) for ph in phases)
    n_steps = sum(reach - 1 for _, reach in scan_strides(n_point))
    field = pltpu.VMEM((n_comp, n_cols, n_point), jnp.float32)
    dma = pltpu.SemaphoreType.DMA
    f32 = jnp.float32
    inputs = (forcing.reshape(n_comp, n_cols, n_point), block_inverse, wall_rates, span_couple)
    out = pl.pallas_call(
        functools.partial(kernel, n_line, n_tile, n_chunk, phases, scale_value),
        out_shape=pltpu.VMEM((n_comp, n_cols, n_point), f32),
        in_specs=[pl.BlockSpec(memory_space=pltpu.HBM)] * 4,
        out_specs=pl.BlockSpec(memory_space=pltpu.VMEM),
        scratch_shapes=[
            field,
            pltpu.VMEM(block_inverse.shape, f32),
            pltpu.VMEM(wall_rates.shape, f32),
            pltpu.SMEM(span_couple.shape, f32),
            dma((4,)),
        ]
        + [field] * 7
        + [
            pltpu.VMEM((n_cols, n_point), f32),
            pltpu.VMEM((n_cols, n_point), f32),
            pltpu.VMEM((2, n_cols, n_point), f32),
            pltpu.VMEM((2, n_line - 1, n_cols, n_point), f32),
            pltpu.VMEM((n_cols, n_point), f32),
            pltpu.VMEM((2, ROWS, n_point), f32),
            pltpu.VMEM((n_line - 1, 2, ROWS, n_point), f32),
            pltpu.VMEM((2, n_steps, n_comp, 1, n_point), f32),
            pltpu.VMEM((2, n_comp, 1, n_point), f32),
            pltpu.VMEM((n_comp, n_cols, n_point), jnp.bfloat16),
            pltpu.VMEM((n_comp, n_cols, n_point), jnp.bfloat16),
            pltpu.VMEM((n_chunk, len(phases), half, 2 * n_cols), f32),
            pltpu.VMEM((n_chunk, n_gram, half, 2 * n_cols), f32),
            dma((2, n_chunk, 2)),
            dma((2, n_chunk, 2)),
            dma((n_chunk,)),
            dma((n_chunk,)),
            dma((2, n_chunk, n_line - 1)),
            dma((2, n_chunk, n_line - 1)),
            dma((n_line - 1,)),
            dma((n_line - 1,)),
            dma((n_chunk, n_gram)),
            dma((n_chunk, n_gram)),
        ],
        compiler_params=pltpu.CompilerParams(
            collective_id=0, has_side_effects=True, vmem_limit_bytes=32 * 1024 * 1024
        ),
    )(*[pltpu.with_memory_space_constraint(value, pltpu.HBM) for value in inputs])
    return out.reshape(n_comp, n_cols, 1, n_point)


def solution(mesh):
    in_specs = (
        P(None, None, "tile", "line"),
        P(None, None, "tile", "line"),
        P(None, None, "tile", "line"),
        P(),
    )
    out_specs = P(None, None, "tile", "line")
    return jax.shard_map(
        functools.partial(local, mesh.shape["line"], mesh.shape["tile"]),
        mesh=mesh, in_specs=in_specs, out_specs=out_specs, check_vma=False,
    )
```

```python
import functools
import math

import jax
import jax.numpy as jnp
from jax import lax
from jax.experimental import pallas as pl
from jax.experimental.pallas import tpu as pltpu
from jax.sharding import PartitionSpec as P

MESH = pl.DeviceIdType.MESH
ROWS = 8


def reduce_phases(n_line, n_tile):
    pair = 2 if n_tile % 2 == 0 else 1
    phases = [(1, pair, True)]
    stride, rest = pair, n_tile // pair
    while rest > 1:
        factor = 4 if rest % 4 == 0 else next(f for f in range(2, rest + 1) if rest % f == 0)
        phases.append((stride, factor, False))
        stride, rest = stride * factor, rest // factor
    return phases


def phase_peers(phase, n_line):
    stride, factor, with_line = phase
    lines = n_line if with_line else 1
    return [(a, b) for a in range(lines) for b in range(factor) if (a, b) != (0, 0)]


def peer_id(phase, step, n_line):
    stride, factor, _ = phase
    line, tile = lax.axis_index("line"), lax.axis_index("tile")
    digit = lax.rem(lax.div(tile, stride), factor)
    there = lax.rem(digit + step[1], factor)
    return (lax.rem(line + step[0], n_line), tile + (there - digit) * stride)


def scan_strides(n_point):
    strides, by = [], 1
    while by < n_point:
        reach = min(4, -(-n_point // by))
        strides.append((by, reach))
        by *= reach
    return strides


def chunk_widths(n_cols):
    return [n_cols // 2, n_cols // 4, n_cols // 4]


def split(value):
    high = value.astype(jnp.bfloat16)
    low = (value - high.astype(jnp.float32)).astype(jnp.bfloat16)
    return high, low


def inverse_of(value):
    guess = pl.reciprocal(value, approx=True)
    guess = guess * (2.0 - value * guess)
    return guess * (2.0 - value * guess)


def eliminate(square, right):
    n, shape = square.shape[0], (ROWS, right.shape[1])
    groups = n // ROWS
    sub = lax.broadcasted_iota(jnp.int32, shape, 0)

    def every(block, at):
        return jnp.broadcast_to(block[at : at + 1], shape)

    blocks = [right[v * ROWS : (v + 1) * ROWS] for v in range(groups)]
    cols = [
        [
            jnp.broadcast_to(square[v * ROWS : (v + 1) * ROWS, e : e + 1], shape)
            for e in range((v + 1) * ROWS)
        ]
        for v in range(groups)
    ]
    for q in range(groups):
        base = q * ROWS
        cell = {(i, j): every(cols[q][base + j], i) for i in range(ROWS) for j in range(i + 1)}
        lines = [every(blocks[q], i) for i in range(ROWS)]
        later = range(q + 1, groups)
        shares = {}
        for c in range(ROWS):
            inv = inverse_of(cell[c, c])
            for i in range(c + 1, ROWS):
                share = cell[i, c] * inv
                for j in range(c + 1, i + 1):
                    cell[i, j] = cell[i, j] - share * cell[j, c]
                lines[i] = lines[i] - share * lines[c]
            for v in later:
                share = cols[v][base + c] * inv
                shares[v, c] = share
                for j in range(c + 1, ROWS):
                    cols[v][base + j] = cols[v][base + j] - share * cell[j, c]
                blocks[v] = blocks[v] - share * lines[c]
        done = lines[0] * lax.rsqrt(cell[0, 0])
        for i in range(1, ROWS):
            done = jnp.where(sub == i, lines[i] * lax.rsqrt(cell[i, i]), done)
        blocks[q] = done
        for w in later:
            for c in range(ROWS):
                for e in range(ROWS):
                    top = every(cols[w][base + c], e)
                    for v in range(w, groups):
                        at = w * ROWS + e
                        cols[v][at] = cols[v][at] - shares[v, c] * top
    return jnp.concatenate(blocks, axis=0)


def kernel(
    n_line, n_tile, widths, phases, scale_value,
    f_in, a_in, w_in, s_in, o_ref,
    f_ref, a_ref, w_ref, s_ref, load_sem,
    start, z_low, z_high, rise, y_low, y_high, fall,
    edge_out, edge_in, ends_out, ends_in, enter, rates_out, rates_in, steps, whole,
    high, low, gram_out, gram_in, halo_send, halo_recv, edge_send, edge_recv, ends_send, ends_recv,
    rates_send, rates_recv, gram_send, gram_recv,
):
    loads = [
        pltpu.make_async_copy(src, dst, load_sem.at[i])
        for i, (src, dst) in enumerate(
            ((f_in, f_ref), (a_in, a_ref), (w_in, w_ref), (s_in, s_ref))
        )
    ]
    for load in loads:
        load.start()
    n_comp, n_cols, n_point = f_ref.shape
    n_chunk = len(widths)
    begins = [sum(widths[:c]) for c in range(n_chunk)]
    ends_at = [sum(widths[: c + 1]) for c in range(n_chunk)]
    line, tile = lax.axis_index("line"), lax.axis_index("tile")
    above, below = lax.rem(tile + 1, n_tile), lax.rem(tile + n_tile - 1, n_tile)
    line_peers = [(lax.rem(line + d, n_line), tile) for d in range(1, n_line)]
    lower_line = (lax.rem(line + n_line - 1, n_line), tile)
    gram_peers = [[peer_id(ph, step, n_line) for step in phase_peers(ph, n_line)] for ph in phases]

    greet = [(line, above), (line, below)] + [p for peers in gram_peers for p in peers]
    barrier = pltpu.get_barrier_semaphore()
    for peer in greet:
        pl.semaphore_signal(barrier, inc=1, device_id=peer, device_id_type=MESH)

    started = []

    def send(src, dst, send_sem, recv_sem, peer):
        copy = pltpu.make_async_remote_copy(
            src_ref=src, dst_ref=dst, send_sem=send_sem, recv_sem=recv_sem,
            device_id=peer, device_id_type=MESH,
        )
        copy.start()
        started.append(copy)
        return copy

    def cut(c):
        return pl.ds(begins[c], widths[c])

    lane3 = lax.broadcasted_iota(jnp.int32, (n_comp, 1, n_point), 2)
    lane8 = lax.broadcasted_iota(jnp.int32, (ROWS, n_point), 1)
    strides = scan_strides(n_point)

    def turn(value, by):
        flat = value.reshape(-1, n_point)
        return pltpu.roll(flat, by % n_point, 1).reshape(value.shape)

    def apply_block(value):
        total = a_ref[:, 0] * value[0][None]
        for m in range(1, n_comp):
            total = total + a_ref[:, m] * value[m][None]
        return total

    def pack(value, at):
        packed = jnp.zeros((value.shape[1], n_point), jnp.float32)
        places = lax.broadcasted_iota(jnp.int32, packed.shape, 1)
        for k in range(n_comp):
            packed = jnp.where(places == k, value[k][:, at : at + 1], packed)
        return packed

    def spread(packed):
        return jnp.stack(
            [jnp.broadcast_to(packed[:, k : k + 1], packed.shape) for k in range(n_comp)], axis=0
        )

    def sweep(value, side):
        slot = 0
        for by, reach in strides:
            parts = [turn(value, -by * m if side else by * m) for m in range(1, reach)]
            for part in parts:
                value = value + steps[side, slot] * part
                slot += 1
        return value

    halos = {}
    edges, ends, rates = [], {}, []

    def send_halo(which, c, field, low, high):
        halos[which, c] = [
            send(field.at[:, cut(c)], low.at[:, cut(c)], halo_send.at[which, c, 0],
                 halo_recv.at[which, c, 0], (line, above)),
            send(field.at[:, cut(c)], high.at[:, cut(c)], halo_send.at[which, c, 1],
                 halo_recv.at[which, c, 1], (line, below)),
        ]

    def send_ends(which, c):
        ends[which, c] = [
            send(ends_out.at[which, cut(c)], ends_in.at[which, d, cut(c)], ends_send.at[which, c, d],
                 ends_recv.at[which, c, d], peer)
            for d, peer in enumerate(line_peers)
        ]

    for load in loads:
        load.wait()
    for c in range(n_chunk):
        field = apply_block(f_ref[:, begins[c] : ends_at[c]])
        start[:, cut(c)] = field
        edge_out[cut(c)] = pack(field, 0)
        if c == 0:
            pl.semaphore_wait(barrier, len(greet))
        send_halo(0, c, start, z_low, z_high)
        edges.append(
            send(edge_out.at[cut(c)], edge_in.at[cut(c)], edge_send.at[c], edge_recv.at[c], lower_line)
        )

    for side in range(2):
        rate = w_ref[side]
        slot = 0
        for by, reach in strides:
            parts = [rate]
            for m in range(1, reach):
                inside = lane3 < n_point - by * m if side else lane3 >= by * m
                steps[side, slot] = jnp.where(inside, rate, 0.0)
                slot += 1
                rate = rate * jnp.where(inside, turn(parts[0], -by * m if side else by * m), 1.0)
        whole[side] = rate
        at = 0 if side else n_point - 1
        total = jnp.zeros((ROWS, n_point), jnp.float32)
        for k in range(n_comp):
            total = jnp.where(lane8 == k, rate[k][:, at : at + 1], total)
        rates_out[side] = total
    for d, peer in enumerate(line_peers):
        rates.append(send(rates_out, rates_in.at[d], rates_send.at[d], rates_recv.at[d], peer))

    def coupled(c, low, high):
        beside = low[:, begins[c] : ends_at[c]] + high[:, begins[c] : ends_at[c]]
        return jnp.stack(
            [f_ref[k, begins[c] : ends_at[c]] + s_ref[k] * beside[k] for k in range(n_comp)], axis=0
        )

    def entry(which, c):
        for copy in ends[which, c]:
            copy.wait_recv()
        total = jnp.zeros((widths[c], n_point), jnp.float32)
        carried = jnp.ones((1, n_point), jnp.float32)
        for d in range(1, n_line):
            slot = n_line - d - 1 if which else d - 1
            reached = (line + d < n_line) if which else (line >= d)
            reached = reached.astype(jnp.float32)
            total = total + (carried * reached) * ends_in[which, slot, cut(c)]
            carried = carried * rates_in[slot, which, 0:1]
        return total

    def first(c):
        for copy in halos[0, c] + [edges[c]]:
            copy.wait_recv()
        source = apply_block(coupled(c, z_low, z_high))
        last = (line < n_line - 1).astype(jnp.float32)
        over = jnp.where(
            lane3 == n_point - 1, spread(edge_in[cut(c)] * last),
            turn(start[:, begins[c] : ends_at[c]], -1),
        )
        value = sweep(source + w_ref[1] * over, 0)
        rise[:, cut(c)] = value
        ends_out[0, cut(c)] = pack(value, n_point - 1)
        send_ends(0, c)

    def first_entry(c):
        if c == 0:
            for copy in rates:
                copy.wait_recv()
        total = entry(0, c)
        enter[cut(c)] = total
        rise[:, cut(c)] = rise[:, cut(c)] + whole[0] * spread(total)
        send_halo(1, c, rise, y_low, y_high)

    def second(c):
        for copy in halos[1, c]:
            copy.wait_recv()
        source = apply_block(coupled(c, y_low, y_high))
        under = jnp.where(
            lane3 == 0, spread(enter[cut(c)]), turn(rise[:, begins[c] : ends_at[c]], 1)
        )
        value = sweep(source + w_ref[0] * under, 1)
        fall[:, cut(c)] = value
        ends_out[1, cut(c)] = pack(value, 0)
        send_ends(1, c)

    def second_entry(c):
        fall[:, cut(c)] = fall[:, cut(c)] + whole[1] * spread(entry(1, c))

    def panel(c):
        wide, till = widths[c], ends_at[c]
        parts = [split(fall[k, cut(c)]) for k in range(n_comp)]
        for k, (top, rest) in enumerate(parts):
            high[k, cut(c)], low[k, cut(c)] = top, rest
        tops = jnp.concatenate([top for top, _ in parts], axis=1)
        left = jnp.concatenate([tops, jnp.concatenate([rest for _, rest in parts], axis=1)], axis=0)
        both = lax.dot_general(
            left, jnp.concatenate([high[k, :till] for k in range(n_comp)], axis=1),
            (((1,), (1,)), ((), ())), preferred_element_type=jnp.float32,
        )
        cross = lax.dot_general(
            tops, jnp.concatenate([low[k, :till] for k in range(n_comp)], axis=1),
            (((1,), (1,)), ((), ())), preferred_element_type=jnp.float32,
        )
        rows = both[:wide] + both[wide:] + cross
        if till < n_cols:
            rows = jnp.concatenate([rows, jnp.zeros((wide, n_cols - till), jnp.float32)], axis=1)
        return jnp.concatenate([rows[: wide // 2], rows[wide // 2 :]], axis=1)

    sums, flights, factor_rows = {}, {}, []

    def gram_send_phase(c, i):
        rows = pl.ds(0, widths[c] // 2)
        gram_out[c, i, rows] = sums[c]
        slot = sum(len(peers) for peers in gram_peers[:i])
        flights[c] = []
        for j, peer in enumerate(gram_peers[i]):
            at = slot + j
            copy = send(gram_out.at[c, i, rows], gram_in.at[c, at, rows], gram_send.at[c, at],
                        gram_recv.at[c, at], peer)
            flights[c].append((copy, at))

    def gram_collect(c):
        for copy, at in flights[c]:
            copy.wait_recv()
            sums[c] = sums[c] + gram_in[c, at, : widths[c] // 2]

    def dot(left, right, transposed):
        return lax.dot_general(
            left, right, (((1,), (1 if transposed else 0,)), ((), ())),
            precision=lax.Precision.HIGHEST, preferred_element_type=jnp.float32,
        )

    def factor(c):
        wide, from_col, till = widths[c], begins[c], ends_at[c]
        rows = jnp.concatenate([sums[c][:, :n_cols], sums[c][:, n_cols:]], axis=0)
        square = rows[:, from_col:till]
        row = lax.broadcasted_iota(jnp.int32, (wide, n_cols), 0)
        col = lax.broadcasted_iota(jnp.int32, (wide, n_cols), 1)
        right = (col == row + from_col).astype(jnp.float32)
        if c:
            known = jnp.concatenate(factor_rows, axis=0)
            lower = dot(rows, known, True)
            square = square - dot(lower, lower, True)
            right = right - dot(lower, known, False)
        factor_rows.append(eliminate(square, right))
        top, rest = split(factor_rows[c][:, :till] * scale_value)
        left = jnp.concatenate([top, rest], axis=0)
        for k in range(n_comp):
            both = jnp.dot(left, high[k, :till], preferred_element_type=jnp.float32)
            cross = jnp.dot(top, low[k, :till], preferred_element_type=jnp.float32)
            o_ref[k, cut(c)] = both[:wide] + both[wide:] + cross

    for c in range(n_chunk):
        first(c)
        if c:
            first_entry(c - 1)
    first_entry(n_chunk - 1)

    def stage(c, which):
        if which == 0:
            second(c)
            return
        if which == 1:
            second_entry(c)
            sums[c] = panel(c)
        else:
            gram_collect(c)
        if which <= len(phases):
            gram_send_phase(c, which - 1)
        else:
            factor(c)

    n_stages = len(phases) + 2
    for now in range(n_chunk + n_stages - 1):
        for c in range(min(now, n_chunk - 1), -1, -1):
            if now - c < n_stages:
                stage(c, now - c)
    for copy in started:
        copy.wait_send()


def local(n_line, n_tile, forcing, block_inverse, wall_rates, span_couple):
    n_comp, n_cols, n_station, n_point = forcing.shape
    assert n_station == 1
    scale_value = math.sqrt(n_comp * n_station * n_tile * n_point * n_line)
    widths = chunk_widths(n_cols)
    n_chunk, half = len(widths), max(widths) // 2
    phases = reduce_phases(n_line, n_tile)
    n_gram = sum(len(phase_peers(ph, n_line)) for ph in phases)
    n_steps = sum(reach - 1 for _, reach in scan_strides(n_point))
    field = pltpu.VMEM((n_comp, n_cols, n_point), jnp.float32)
    dma = pltpu.SemaphoreType.DMA
    f32 = jnp.float32
    inputs = (forcing.reshape(n_comp, n_cols, n_point), block_inverse, wall_rates, span_couple)
    out = pl.pallas_call(
        functools.partial(kernel, n_line, n_tile, widths, phases, scale_value),
        out_shape=pltpu.VMEM((n_comp, n_cols, n_point), f32),
        in_specs=[pl.BlockSpec(memory_space=pltpu.HBM)] * 4,
        out_specs=pl.BlockSpec(memory_space=pltpu.VMEM),
        scratch_shapes=[
            field,
            pltpu.VMEM(block_inverse.shape, f32),
            pltpu.VMEM(wall_rates.shape, f32),
            pltpu.SMEM(span_couple.shape, f32),
            dma((4,)),
        ]
        + [field] * 7
        + [
            pltpu.VMEM((n_cols, n_point), f32),
            pltpu.VMEM((n_cols, n_point), f32),
            pltpu.VMEM((2, n_cols, n_point), f32),
            pltpu.VMEM((2, n_line - 1, n_cols, n_point), f32),
            pltpu.VMEM((n_cols, n_point), f32),
            pltpu.VMEM((2, ROWS, n_point), f32),
            pltpu.VMEM((n_line - 1, 2, ROWS, n_point), f32),
            pltpu.VMEM((2, n_steps, n_comp, 1, n_point), f32),
            pltpu.VMEM((2, n_comp, 1, n_point), f32),
            pltpu.VMEM((n_comp, n_cols, n_point), jnp.bfloat16),
            pltpu.VMEM((n_comp, n_cols, n_point), jnp.bfloat16),
            pltpu.VMEM((n_chunk, len(phases), half, 2 * n_cols), f32),
            pltpu.VMEM((n_chunk, n_gram, half, 2 * n_cols), f32),
            dma((2, n_chunk, 2)),
            dma((2, n_chunk, 2)),
            dma((n_chunk,)),
            dma((n_chunk,)),
            dma((2, n_chunk, n_line - 1)),
            dma((2, n_chunk, n_line - 1)),
            dma((n_line - 1,)),
            dma((n_line - 1,)),
            dma((n_chunk, n_gram)),
            dma((n_chunk, n_gram)),
        ],
        compiler_params=pltpu.CompilerParams(
            collective_id=0, has_side_effects=True, vmem_limit_bytes=32 * 1024 * 1024
        ),
    )(*[pltpu.with_memory_space_constraint(value, pltpu.HBM) for value in inputs])
    return out.reshape(n_comp, n_cols, 1, n_point)


def solution(mesh):
    in_specs = (
        P(None, None, "tile", "line"),
        P(None, None, "tile", "line"),
        P(None, None, "tile", "line"),
        P(),
    )
    out_specs = P(None, None, "tile", "line")
    return jax.shard_map(
        functools.partial(local, mesh.shape["line"], mesh.shape["tile"]),
        mesh=mesh, in_specs=in_specs, out_specs=out_specs, check_vma=False,
    )
```

```python
import functools
import math

import jax
import jax.numpy as jnp
from jax import lax
from jax.experimental import pallas as pl
from jax.experimental.pallas import tpu as pltpu
from jax.sharding import PartitionSpec as P

MESH = pl.DeviceIdType.MESH
ROWS = 8


def reduce_phases(n_line, n_tile):
    pair = 2 if n_tile % 2 == 0 else 1
    phases = [(1, pair, True)]
    stride, rest = pair, n_tile // pair
    while rest > 1:
        factor = 4 if rest % 4 == 0 else next(f for f in range(2, rest + 1) if rest % f == 0)
        phases.append((stride, factor, False))
        stride, rest = stride * factor, rest // factor
    return phases


def phase_peers(phase, n_line):
    stride, factor, with_line = phase
    lines = n_line if with_line else 1
    return [(a, b) for a in range(lines) for b in range(factor) if (a, b) != (0, 0)]


def peer_id(phase, step, n_line):
    stride, factor, _ = phase
    line, tile = lax.axis_index("line"), lax.axis_index("tile")
    digit = lax.rem(lax.div(tile, stride), factor)
    there = lax.rem(digit + step[1], factor)
    return (lax.rem(line + step[0], n_line), tile + (there - digit) * stride)


def scan_strides(n_point):
    strides, by = [], 1
    while by < n_point:
        reach = min(4, -(-n_point // by))
        strides.append((by, reach))
        by *= reach
    return strides


def chunk_widths(n_cols):
    return [n_cols // 2, n_cols // 2]


def split(value):
    high = value.astype(jnp.bfloat16)
    low = (value - high.astype(jnp.float32)).astype(jnp.bfloat16)
    return high, low


def inverse_of(value):
    guess = pl.reciprocal(value, approx=True)
    guess = guess * (2.0 - value * guess)
    return guess * (2.0 - value * guess)


def eliminate(square, right):
    n, shape = square.shape[0], (ROWS, right.shape[1])
    groups = n // ROWS
    sub = lax.broadcasted_iota(jnp.int32, shape, 0)

    def every(block, at):
        return jnp.broadcast_to(block[at : at + 1], shape)

    blocks = [right[v * ROWS : (v + 1) * ROWS] for v in range(groups)]
    cols = [
        [
            jnp.broadcast_to(square[v * ROWS : (v + 1) * ROWS, e : e + 1], shape)
            for e in range((v + 1) * ROWS)
        ]
        for v in range(groups)
    ]
    for q in range(groups):
        base = q * ROWS
        cell = {(i, j): every(cols[q][base + j], i) for i in range(ROWS) for j in range(i + 1)}
        lines = [every(blocks[q], i) for i in range(ROWS)]
        later = range(q + 1, groups)
        shares = {}
        for c in range(ROWS):
            inv = inverse_of(cell[c, c])
            for i in range(c + 1, ROWS):
                share = cell[i, c] * inv
                for j in range(c + 1, i + 1):
                    cell[i, j] = cell[i, j] - share * cell[j, c]
                lines[i] = lines[i] - share * lines[c]
            for v in later:
                share = cols[v][base + c] * inv
                shares[v, c] = share
                for j in range(c + 1, ROWS):
                    cols[v][base + j] = cols[v][base + j] - share * cell[j, c]
                blocks[v] = blocks[v] - share * lines[c]
        done = lines[0] * lax.rsqrt(cell[0, 0])
        for i in range(1, ROWS):
            done = jnp.where(sub == i, lines[i] * lax.rsqrt(cell[i, i]), done)
        blocks[q] = done
        for w in later:
            for c in range(ROWS):
                for e in range(ROWS):
                    top = every(cols[w][base + c], e)
                    for v in range(w, groups):
                        at = w * ROWS + e
                        cols[v][at] = cols[v][at] - shares[v, c] * top
    return jnp.concatenate(blocks, axis=0)


def kernel(
    n_line, n_tile, widths, phases, scale_value,
    f_in, a_in, w_in, s_in, o_ref,
    f_ref, a_ref, w_ref, s_ref, load_sem,
    start, z_low, z_high, rise, y_low, y_high, fall,
    edge_out, edge_in, ends_out, ends_in, enter, rates_out, rates_in, steps, whole,
    high, low, gram_out, gram_in, halo_send, halo_recv, edge_send, edge_recv, ends_send, ends_recv,
    rates_send, rates_recv, gram_send, gram_recv,
):
    loads = [
        pltpu.make_async_copy(src, dst, load_sem.at[i])
        for i, (src, dst) in enumerate(
            ((f_in, f_ref), (a_in, a_ref), (w_in, w_ref), (s_in, s_ref))
        )
    ]
    for load in loads:
        load.start()
    n_comp, n_cols, n_point = f_ref.shape
    n_chunk = len(widths)
    begins = [sum(widths[:c]) for c in range(n_chunk)]
    ends_at = [sum(widths[: c + 1]) for c in range(n_chunk)]
    line, tile = lax.axis_index("line"), lax.axis_index("tile")
    above, below = lax.rem(tile + 1, n_tile), lax.rem(tile + n_tile - 1, n_tile)
    line_peers = [(lax.rem(line + d, n_line), tile) for d in range(1, n_line)]
    lower_line = (lax.rem(line + n_line - 1, n_line), tile)
    gram_peers = [[peer_id(ph, step, n_line) for step in phase_peers(ph, n_line)] for ph in phases]

    ends_in[...] = jnp.zeros(ends_in.shape, jnp.float32)
    greet = [(line, above), (line, below)] + [p for peers in gram_peers for p in peers]
    barrier = pltpu.get_barrier_semaphore()
    for peer in greet:
        pl.semaphore_signal(barrier, inc=1, device_id=peer, device_id_type=MESH)

    started = []

    def send(src, dst, send_sem, recv_sem, peer):
        copy = pltpu.make_async_remote_copy(
            src_ref=src, dst_ref=dst, send_sem=send_sem, recv_sem=recv_sem,
            device_id=peer, device_id_type=MESH,
        )
        copy.start()
        started.append(copy)
        return copy

    def cut(c):
        return pl.ds(begins[c], widths[c])

    lane3 = lax.broadcasted_iota(jnp.int32, (n_comp, 1, n_point), 2)
    lane8 = lax.broadcasted_iota(jnp.int32, (ROWS, n_point), 1)
    strides = scan_strides(n_point)

    def turn(value, by):
        flat = value.reshape(-1, n_point)
        return pltpu.roll(flat, by % n_point, 1).reshape(value.shape)

    def apply_block(value):
        total = a_ref[:, 0] * value[0][None]
        for m in range(1, n_comp):
            total = total + a_ref[:, m] * value[m][None]
        return total

    def pack(value, at):
        packed = jnp.zeros((value.shape[1], n_point), jnp.float32)
        places = lax.broadcasted_iota(jnp.int32, packed.shape, 1)
        for k in range(n_comp):
            packed = jnp.where(places == k, value[k][:, at : at + 1], packed)
        return packed

    def spread(packed):
        return jnp.stack(
            [jnp.broadcast_to(packed[:, k : k + 1], packed.shape) for k in range(n_comp)], axis=0
        )

    def sweep(value, side):
        slot = 0
        for by, reach in strides:
            parts = [turn(value, -by * m if side else by * m) for m in range(1, reach)]
            for part in parts:
                value = value + steps[side, slot] * part
                slot += 1
        return value

    halos = {}
    edges, rates = [], []

    def send_halo(which, c, field, low, high):
        halos[which, c] = [
            send(field.at[:, cut(c)], low.at[:, cut(c)], halo_send.at[which, c, 0],
                 halo_recv.at[which, c, 0], (line, above)),
            send(field.at[:, cut(c)], high.at[:, cut(c)], halo_send.at[which, c, 1],
                 halo_recv.at[which, c, 1], (line, below)),
        ]

    def ends_copy(which, c, d):
        return pltpu.make_async_remote_copy(
            src_ref=ends_out.at[which, cut(c)], dst_ref=ends_in.at[which, d, cut(c)],
            send_sem=ends_send.at[which, c, d], recv_sem=ends_recv.at[which, c, d],
            device_id=line_peers[d], device_id_type=MESH,
        )

    def reaches(which, d):
        if which:
            return line + d + 1 >= n_line, line + n_line - d - 1 < n_line
        return line + d + 1 < n_line, line >= d + 1

    def send_ends(which, c):
        for d in range(n_line - 1):
            @pl.when(reaches(which, d)[0])
            def _():
                ends_copy(which, c, d).start()

    def wait_ends(which, c, sent):
        for d in range(n_line - 1):
            @pl.when(reaches(which, d)[0 if sent else 1])
            def _():
                copy = ends_copy(which, c, d)
                copy.wait_send() if sent else copy.wait_recv()

    for load in loads:
        load.wait()
    for c in range(n_chunk):
        field = apply_block(f_ref[:, begins[c] : ends_at[c]])
        start[:, cut(c)] = field
        edge_out[cut(c)] = pack(field, 0)
        if c == 0:
            pl.semaphore_wait(barrier, len(greet))
        send_halo(0, c, start, z_low, z_high)
        edges.append(
            send(edge_out.at[cut(c)], edge_in.at[cut(c)], edge_send.at[c], edge_recv.at[c], lower_line)
        )

    for side in range(2):
        rate = w_ref[side]
        slot = 0
        for by, reach in strides:
            parts = [rate]
            for m in range(1, reach):
                inside = lane3 < n_point - by * m if side else lane3 >= by * m
                steps[side, slot] = jnp.where(inside, rate, 0.0)
                slot += 1
                rate = rate * jnp.where(inside, turn(parts[0], -by * m if side else by * m), 1.0)
        whole[side] = rate
        at = 0 if side else n_point - 1
        total = jnp.zeros((ROWS, n_point), jnp.float32)
        for k in range(n_comp):
            total = jnp.where(lane8 == k, rate[k][:, at : at + 1], total)
        rates_out[side] = total
    for d, peer in enumerate(line_peers):
        rates.append(send(rates_out, rates_in.at[d], rates_send.at[d], rates_recv.at[d], peer))

    def coupled(c, low, high):
        beside = low[:, begins[c] : ends_at[c]] + high[:, begins[c] : ends_at[c]]
        return jnp.stack(
            [f_ref[k, begins[c] : ends_at[c]] + s_ref[k] * beside[k] for k in range(n_comp)], axis=0
        )

    def entry(which, c):
        wait_ends(which, c, False)
        total = jnp.zeros((widths[c], n_point), jnp.float32)
        carried = jnp.ones((1, n_point), jnp.float32)
        for d in range(1, n_line):
            slot = n_line - d - 1 if which else d - 1
            total = total + carried * ends_in[which, slot, cut(c)]
            carried = carried * rates_in[slot, which, 0:1]
        return total

    def first(c):
        for copy in halos[0, c] + [edges[c]]:
            copy.wait_recv()
        source = apply_block(coupled(c, z_low, z_high))
        last = (line < n_line - 1).astype(jnp.float32)
        over = jnp.where(
            lane3 == n_point - 1, spread(edge_in[cut(c)] * last),
            turn(start[:, begins[c] : ends_at[c]], -1),
        )
        value = sweep(source + w_ref[1] * over, 0)
        rise[:, cut(c)] = value
        ends_out[0, cut(c)] = pack(value, n_point - 1)
        send_ends(0, c)

    def first_entry(c):
        if c == 0:
            for copy in rates:
                copy.wait_recv()
        total = entry(0, c)
        enter[cut(c)] = total
        rise[:, cut(c)] = rise[:, cut(c)] + whole[0] * spread(total)
        send_halo(1, c, rise, y_low, y_high)

    def second(c):
        for copy in halos[1, c]:
            copy.wait_recv()
        source = apply_block(coupled(c, y_low, y_high))
        under = jnp.where(
            lane3 == 0, spread(enter[cut(c)]), turn(rise[:, begins[c] : ends_at[c]], 1)
        )
        value = sweep(source + w_ref[0] * under, 1)
        fall[:, cut(c)] = value
        ends_out[1, cut(c)] = pack(value, 0)
        send_ends(1, c)

    def second_entry(c):
        fall[:, cut(c)] = fall[:, cut(c)] + whole[1] * spread(entry(1, c))

    def panel(c):
        wide, till = widths[c], ends_at[c]
        parts = [split(fall[k, cut(c)]) for k in range(n_comp)]
        for k, (top, rest) in enumerate(parts):
            high[k, cut(c)], low[k, cut(c)] = top, rest
        tops = jnp.concatenate([top for top, _ in parts], axis=1)
        left = jnp.concatenate([tops, jnp.concatenate([rest for _, rest in parts], axis=1)], axis=0)
        both = lax.dot_general(
            left, jnp.concatenate([high[k, :till] for k in range(n_comp)], axis=1),
            (((1,), (1,)), ((), ())), preferred_element_type=jnp.float32,
        )
        cross = lax.dot_general(
            tops, jnp.concatenate([low[k, :till] for k in range(n_comp)], axis=1),
            (((1,), (1,)), ((), ())), preferred_element_type=jnp.float32,
        )
        rows = both[:wide] + both[wide:] + cross
        if till < n_cols:
            rows = jnp.concatenate([rows, jnp.zeros((wide, n_cols - till), jnp.float32)], axis=1)
        return jnp.concatenate([rows[: wide // 2], rows[wide // 2 :]], axis=1)

    sums, flights, factor_rows = {}, {}, []

    def gram_send_phase(c, i):
        rows = pl.ds(0, widths[c] // 2)
        gram_out[c, i, rows] = sums[c]
        slot = sum(len(peers) for peers in gram_peers[:i])
        flights[c] = []
        for j, peer in enumerate(gram_peers[i]):
            at = slot + j
            copy = send(gram_out.at[c, i, rows], gram_in.at[c, at, rows], gram_send.at[c, at],
                        gram_recv.at[c, at], peer)
            flights[c].append((copy, at))

    def gram_collect(c):
        for copy, at in flights[c]:
            copy.wait_recv()
            sums[c] = sums[c] + gram_in[c, at, : widths[c] // 2]

    def dot(left, right, transposed):
        return lax.dot_general(
            left, right, (((1,), (1 if transposed else 0,)), ((), ())),
            precision=lax.Precision.HIGHEST, preferred_element_type=jnp.float32,
        )

    def factor(c):
        wide, from_col, till = widths[c], begins[c], ends_at[c]
        rows = jnp.concatenate([sums[c][:, :n_cols], sums[c][:, n_cols:]], axis=0)
        square = rows[:, from_col:till]
        row = lax.broadcasted_iota(jnp.int32, (wide, n_cols), 0)
        col = lax.broadcasted_iota(jnp.int32, (wide, n_cols), 1)
        right = (col == row + from_col).astype(jnp.float32)
        if c:
            known = jnp.concatenate(factor_rows, axis=0)
            lower = dot(rows, known, True)
            square = square - dot(lower, lower, True)
            right = right - dot(lower, known, False)
        factor_rows.append(eliminate(square, right))
        top, rest = split(factor_rows[c][:, :till] * scale_value)
        left = jnp.concatenate([top, rest], axis=0)
        for k in range(n_comp):
            both = jnp.dot(left, high[k, :till], preferred_element_type=jnp.float32)
            cross = jnp.dot(top, low[k, :till], preferred_element_type=jnp.float32)
            o_ref[k, cut(c)] = both[:wide] + both[wide:] + cross

    def drain(keep):
        while len(started) > keep:
            started.pop(0).wait_send()

    for c in range(n_chunk):
        first(c)
        first_entry(c)

    def stage(c, which):
        if which:
            if c == n_chunk - 1:
                drain(len(flights[c]))
                if which == 1:
                    for side in range(2):
                        for part in range(n_chunk):
                            wait_ends(side, part, True)
            gram_collect(c)
        if which < len(phases):
            gram_send_phase(c, which)
        else:
            factor(c)

    for now in range(n_chunk + len(phases)):
        if now < n_chunk:
            second(now)
        for c in range(min(now, n_chunk)):
            if now - c <= len(phases):
                stage(c, now - c)
        if now < n_chunk:
            second_entry(now)
            sums[now] = panel(now)
            stage(now, 0)
    drain(0)


def local(n_line, n_tile, forcing, block_inverse, wall_rates, span_couple):
    n_comp, n_cols, n_station, n_point = forcing.shape
    assert n_station == 1
    scale_value = math.sqrt(n_comp * n_station * n_tile * n_point * n_line)
    widths = chunk_widths(n_cols)
    n_chunk, half = len(widths), max(widths) // 2
    phases = reduce_phases(n_line, n_tile)
    n_gram = sum(len(phase_peers(ph, n_line)) for ph in phases)
    n_steps = sum(reach - 1 for _, reach in scan_strides(n_point))
    field = pltpu.VMEM((n_comp, n_cols, n_point), jnp.float32)
    dma = pltpu.SemaphoreType.DMA
    f32 = jnp.float32
    inputs = (forcing.reshape(n_comp, n_cols, n_point), block_inverse, wall_rates, span_couple)
    out = pl.pallas_call(
        functools.partial(kernel, n_line, n_tile, widths, phases, scale_value),
        out_shape=pltpu.VMEM((n_comp, n_cols, n_point), f32),
        in_specs=[pl.BlockSpec(memory_space=pltpu.HBM)] * 4,
        out_specs=pl.BlockSpec(memory_space=pltpu.VMEM),
        scratch_shapes=[
            field,
            pltpu.VMEM(block_inverse.shape, f32),
            pltpu.VMEM(wall_rates.shape, f32),
            pltpu.SMEM(span_couple.shape, f32),
            dma((4,)),
        ]
        + [field] * 7
        + [
            pltpu.VMEM((n_cols, n_point), f32),
            pltpu.VMEM((n_cols, n_point), f32),
            pltpu.VMEM((2, n_cols, n_point), f32),
            pltpu.VMEM((2, n_line - 1, n_cols, n_point), f32),
            pltpu.VMEM((n_cols, n_point), f32),
            pltpu.VMEM((2, ROWS, n_point), f32),
            pltpu.VMEM((n_line - 1, 2, ROWS, n_point), f32),
            pltpu.VMEM((2, n_steps, n_comp, 1, n_point), f32),
            pltpu.VMEM((2, n_comp, 1, n_point), f32),
            pltpu.VMEM((n_comp, n_cols, n_point), jnp.bfloat16),
            pltpu.VMEM((n_comp, n_cols, n_point), jnp.bfloat16),
            pltpu.VMEM((n_chunk, len(phases), half, 2 * n_cols), f32),
            pltpu.VMEM((n_chunk, n_gram, half, 2 * n_cols), f32),
            dma((2, n_chunk, 2)),
            dma((2, n_chunk, 2)),
            dma((n_chunk,)),
            dma((n_chunk,)),
            dma((2, n_chunk, n_line - 1)),
            dma((2, n_chunk, n_line - 1)),
            dma((n_line - 1,)),
            dma((n_line - 1,)),
            dma((n_chunk, n_gram)),
            dma((n_chunk, n_gram)),
        ],
        compiler_params=pltpu.CompilerParams(
            collective_id=0, has_side_effects=True, vmem_limit_bytes=32 * 1024 * 1024
        ),
    )(*[pltpu.with_memory_space_constraint(value, pltpu.HBM) for value in inputs])
    return out.reshape(n_comp, n_cols, 1, n_point)


def solution(mesh):
    in_specs = (
        P(None, None, "tile", "line"),
        P(None, None, "tile", "line"),
        P(None, None, "tile", "line"),
        P(),
    )
    out_specs = P(None, None, "tile", "line")
    return jax.shard_map(
        functools.partial(local, mesh.shape["line"], mesh.shape["tile"]),
        mesh=mesh, in_specs=in_specs, out_specs=out_specs, check_vma=False,
    )
```

```python
import functools
import math

import jax
import jax.numpy as jnp
from jax import lax
from jax.experimental import pallas as pl
from jax.experimental.pallas import tpu as pltpu
from jax.sharding import PartitionSpec as P

MESH = pl.DeviceIdType.MESH
ROWS = 8


def reduce_phases(n_line, n_tile):
    pair = 2 if n_tile % 2 == 0 else 1
    phases = [(1, pair, True)]
    stride, rest = pair, n_tile // pair
    while rest > 1:
        factor = 4 if rest % 4 == 0 else next(f for f in range(2, rest + 1) if rest % f == 0)
        phases.append((stride, factor, False))
        stride, rest = stride * factor, rest // factor
    return phases


def phase_peers(phase, n_line):
    stride, factor, with_line = phase
    lines = n_line if with_line else 1
    return [(a, b) for a in range(lines) for b in range(factor) if (a, b) != (0, 0)]


def peer_id(phase, step, n_line):
    stride, factor, _ = phase
    line, tile = lax.axis_index("line"), lax.axis_index("tile")
    digit = lax.rem(lax.div(tile, stride), factor)
    there = lax.rem(digit + step[1], factor)
    return (lax.rem(line + step[0], n_line), tile + (there - digit) * stride)


def scan_strides(n_point):
    strides, by = [], 1
    while by < n_point:
        reach = min(4, -(-n_point // by))
        strides.append((by, reach))
        by *= reach
    return strides


def split(value):
    high = value.astype(jnp.bfloat16)
    low = (value - high.astype(jnp.float32)).astype(jnp.bfloat16)
    return high, low


def eliminate(gram):
    n = gram.shape[0]
    row = lax.broadcasted_iota(jnp.int32, (n, n), 0)
    col = lax.broadcasted_iota(jnp.int32, (n, n), 1)
    both = jnp.concatenate([gram, (row == col).astype(jnp.float32)], axis=1)
    blocks = [both[v * ROWS : (v + 1) * ROWS] for v in range(n // ROWS)]
    shape = (ROWS, 2 * n)
    sub = lax.broadcasted_iota(jnp.int32, shape, 0)
    scales = []
    for q in range(n // ROWS):
        live = range(q, n // ROWS)
        cols = [
            {v: jnp.broadcast_to(blocks[v][:, ROWS * q + c : ROWS * q + c + 1], shape) for v in live}
            for c in range(ROWS)
        ]
        scale = jnp.zeros(shape, jnp.float32)
        for c in range(ROWS):
            pivot = jnp.broadcast_to(cols[c][q][c : c + 1], shape)
            inv = 1.0 / pivot
            scale = jnp.where(sub == c, lax.rsqrt(pivot), scale)
            factor = {v: cols[c][v] * inv for v in live}
            factor[q] = jnp.where(sub > c, factor[q], 0.0)
            top = jnp.broadcast_to(blocks[q][c : c + 1], shape)
            tops = [jnp.broadcast_to(cols[e][q][c : c + 1], shape) for e in range(c + 1, ROWS)]
            for v in live:
                blocks[v] = blocks[v] - factor[v] * top
                for e in range(c + 1, ROWS):
                    cols[e][v] = cols[e][v] - factor[v] * tops[e - c - 1]
        scales.append(scale)
    return jnp.concatenate([b * s for b, s in zip(blocks, scales)], axis=0)[:, n:]


def kernel(
    n_line, n_tile, n_chunk, phases, scale_value,
    f_in, a_in, w_in, s_in, o_ref,
    f_ref, a_ref, w_ref, s_ref, load_sem,
    start, z_low, z_high, rise, y_low, y_high, fall,
    edge_out, edge_in, ends_out, ends_in, enter, rates_out, rates_in, steps, whole,
    gram_out, gram_in, halo_send, halo_recv, edge_send, edge_recv, ends_send, ends_recv,
    rates_send, rates_recv, gram_send, gram_recv,
):
    loads = [
        pltpu.make_async_copy(src, dst, load_sem.at[i])
        for i, (src, dst) in enumerate(
            ((f_in, f_ref), (a_in, a_ref), (w_in, w_ref), (s_in, s_ref))
        )
    ]
    for load in loads:
        load.start()
    n_comp, n_cols, n_point = f_ref.shape
    wide = n_cols // n_chunk
    line, tile = lax.axis_index("line"), lax.axis_index("tile")
    above, below = lax.rem(tile + 1, n_tile), lax.rem(tile + n_tile - 1, n_tile)
    line_peers = [(lax.rem(line + d, n_line), tile) for d in range(1, n_line)]
    lower_line = (lax.rem(line + n_line - 1, n_line), tile)
    gram_peers = [[peer_id(ph, step, n_line) for step in phase_peers(ph, n_line)] for ph in phases]

    ends_in[...] = jnp.zeros(ends_in.shape, jnp.float32)
    greet = [(line, above), (line, below)] + [p for peers in gram_peers for p in peers]
    barrier = pltpu.get_barrier_semaphore()
    for peer in greet:
        pl.semaphore_signal(barrier, inc=1, device_id=peer, device_id_type=MESH)

    started = []

    def send(src, dst, send_sem, recv_sem, peer):
        copy = pltpu.make_async_remote_copy(
            src_ref=src, dst_ref=dst, send_sem=send_sem, recv_sem=recv_sem,
            device_id=peer, device_id_type=MESH,
        )
        copy.start()
        started.append(copy)
        return copy

    def cut(c):
        return pl.ds(pl.multiple_of(c * wide, wide), wide)

    lane3 = lax.broadcasted_iota(jnp.int32, (n_comp, 1, n_point), 2)
    lane8 = lax.broadcasted_iota(jnp.int32, (ROWS, n_point), 1)
    strides = scan_strides(n_point)

    def turn(value, by):
        flat = value.reshape(-1, n_point)
        return pltpu.roll(flat, by % n_point, 1).reshape(value.shape)

    def apply_block(value):
        total = a_ref[:, 0] * value[0][None]
        for m in range(1, n_comp):
            total = total + a_ref[:, m] * value[m][None]
        return total

    def pack(value, at):
        packed = jnp.zeros((value.shape[1], n_point), jnp.float32)
        places = lax.broadcasted_iota(jnp.int32, packed.shape, 1)
        for k in range(n_comp):
            packed = jnp.where(places == k, value[k][:, at : at + 1], packed)
        return packed

    def spread(packed):
        return jnp.stack(
            [jnp.broadcast_to(packed[:, k : k + 1], packed.shape) for k in range(n_comp)], axis=0
        )

    def sweep(value, side):
        slot = 0
        for by, reach in strides:
            parts = [turn(value, -by * m if side else by * m) for m in range(1, reach)]
            for part in parts:
                value = value + steps[side, slot] * part
                slot += 1
        return value

    rates = []

    def halo_copies(which, c):
        field, low, high = ((start, z_low, z_high), (rise, y_low, y_high))[which]
        return [
            pltpu.make_async_remote_copy(
                src_ref=field.at[:, cut(c)], dst_ref=there.at[:, cut(c)],
                send_sem=halo_send.at[which, c, side], recv_sem=halo_recv.at[which, c, side],
                device_id=(line, to), device_id_type=MESH,
            )
            for side, (there, to) in enumerate(((low, above), (high, below)))
        ]

    def edge_copy(c):
        return pltpu.make_async_remote_copy(
            src_ref=edge_out.at[cut(c)], dst_ref=edge_in.at[cut(c)], send_sem=edge_send.at[c],
            recv_sem=edge_recv.at[c], device_id=lower_line, device_id_type=MESH,
        )

    def ends_copy(which, c, d):
        return pltpu.make_async_remote_copy(
            src_ref=ends_out.at[which, cut(c)], dst_ref=ends_in.at[which, d, cut(c)],
            send_sem=ends_send.at[which, c, d], recv_sem=ends_recv.at[which, c, d],
            device_id=line_peers[d], device_id_type=MESH,
        )

    def reaches(which, d):
        if which:
            return line + d + 1 >= n_line, line + n_line - d - 1 < n_line
        return line + d + 1 < n_line, line >= d + 1

    def send_ends(which, c):
        for d in range(n_line - 1):
            @pl.when(reaches(which, d)[0])
            def _():
                ends_copy(which, c, d).start()

    def wait_ends(which, c, sent):
        for d in range(n_line - 1):
            @pl.when(reaches(which, d)[0 if sent else 1])
            def _():
                copy = ends_copy(which, c, d)
                copy.wait_send() if sent else copy.wait_recv()

    for load in loads:
        load.wait()
    def begin(c, _):
        field = apply_block(f_ref[:, cut(c)])
        start[:, cut(c)] = field
        edge_out[cut(c)] = pack(field, 0)

        @pl.when(c == 0)
        def _():
            pl.semaphore_wait(barrier, len(greet))

        for copy in halo_copies(0, c) + [edge_copy(c)]:
            copy.start()
        return 0

    lax.fori_loop(0, n_chunk, begin, 0)

    for side in range(2):
        rate = w_ref[side]
        slot = 0
        for by, reach in strides:
            parts = [rate]
            for m in range(1, reach):
                inside = lane3 < n_point - by * m if side else lane3 >= by * m
                steps[side, slot] = jnp.where(inside, rate, 0.0)
                slot += 1
                rate = rate * jnp.where(inside, turn(parts[0], -by * m if side else by * m), 1.0)
        whole[side] = rate
        at = 0 if side else n_point - 1
        total = jnp.zeros((ROWS, n_point), jnp.float32)
        for k in range(n_comp):
            total = jnp.where(lane8 == k, rate[k][:, at : at + 1], total)
        rates_out[side] = total
    for d, peer in enumerate(line_peers):
        rates.append(send(rates_out, rates_in.at[d], rates_send.at[d], rates_recv.at[d], peer))

    def coupled(c, low, high):
        beside = low[:, cut(c)] + high[:, cut(c)]
        return jnp.stack(
            [f_ref[k, cut(c)] + s_ref[k] * beside[k] for k in range(n_comp)], axis=0
        )

    def entry(which, c):
        wait_ends(which, c, False)
        total = jnp.zeros((wide, n_point), jnp.float32)
        carried = jnp.ones((1, n_point), jnp.float32)
        for d in range(1, n_line):
            slot = n_line - d - 1 if which else d - 1
            total = total + carried * ends_in[which, slot, cut(c)]
            carried = carried * rates_in[slot, which, 0:1]
        return total

    def first(c):
        for copy in halo_copies(0, c) + [edge_copy(c)]:
            copy.wait_recv()
        source = apply_block(coupled(c, z_low, z_high))
        last = (line < n_line - 1).astype(jnp.float32)
        over = jnp.where(
            lane3 == n_point - 1, spread(edge_in[cut(c)] * last),
            turn(start[:, cut(c)], -1),
        )
        value = sweep(source + w_ref[1] * over, 0)
        rise[:, cut(c)] = value
        ends_out[0, cut(c)] = pack(value, n_point - 1)
        send_ends(0, c)

    def first_entry(c):
        @pl.when(c == 0)
        def _():
            for copy in rates:
                copy.wait_recv()

        total = entry(0, c)
        enter[cut(c)] = total
        rise[:, cut(c)] = rise[:, cut(c)] + whole[0] * spread(total)
        for copy in halo_copies(1, c):
            copy.start()

    def second(c):
        for copy in halo_copies(1, c):
            copy.wait_recv()
        source = apply_block(coupled(c, y_low, y_high))
        under = jnp.where(
            lane3 == 0, spread(enter[cut(c)]), turn(rise[:, cut(c)], 1)
        )
        value = sweep(source + w_ref[0] * under, 1)
        fall[:, cut(c)] = value
        ends_out[1, cut(c)] = pack(value, 0)
        send_ends(1, c)

    def second_entry(c):
        fall[:, cut(c)] = fall[:, cut(c)] + whole[1] * spread(entry(1, c))

    def sweeps(work, finish):
        def step(c, _):
            @pl.when(c < n_chunk)
            def _():
                work(c)

            @pl.when(c > 0)
            def _():
                finish(c - 1)

            return 0

        lax.fori_loop(0, n_chunk + 1, step, 0)

    sweeps(first, first_entry)
    sweeps(second, second_entry)

    def drain(c, _):
        for copy in halo_copies(0, c) + halo_copies(1, c) + [edge_copy(c)]:
            copy.wait_send()
        for side in range(2):
            wait_ends(side, c, True)
        return 0

    total = jnp.zeros((2 * n_cols, 2 * n_cols), jnp.float32)
    for k in range(n_comp):
        both = jnp.concatenate(split(fall[k]), axis=0)
        total = total + lax.dot_general(
            both, both, (((1,), (1,)), ((), ())), preferred_element_type=jnp.float32
        )
    gram = total[:n_cols] + total[n_cols:]
    gram = gram[:, :n_cols] + gram[:, n_cols:]
    half = n_cols // 2
    packed = jnp.concatenate([gram[:half], gram[half:]], axis=1)
    slot = 0
    for i, peers in enumerate(gram_peers):
        gram_out[i] = packed
        copies = []
        for peer in peers:
            copies.append(
                send(gram_out.at[i], gram_in.at[slot], gram_send.at[slot], gram_recv.at[slot], peer)
            )
            slot += 1
        if i == 0:
            lax.fori_loop(0, n_chunk, drain, 0)
            for copy in rates:
                copy.wait_send()
        for j, copy in enumerate(copies):
            copy.wait_recv()
            packed = packed + gram_in[slot - len(copies) + j]
    gram = jnp.concatenate([packed[:, :n_cols], packed[:, n_cols:]], axis=0)

    high, low = split(eliminate(gram) * scale_value)
    left = jnp.concatenate([high, high, low], axis=1)
    for k in range(n_comp):
        top, rest = split(fall[k])
        o_ref[k] = jnp.dot(
            left, jnp.concatenate([top, rest, top], axis=0), preferred_element_type=jnp.float32
        )
    for copy in started[len(rates) :]:
        copy.wait_send()


def local(n_line, n_tile, forcing, block_inverse, wall_rates, span_couple):
    n_comp, n_cols, n_station, n_point = forcing.shape
    assert n_station == 1
    scale_value = math.sqrt(n_comp * n_station * n_tile * n_point * n_line)
    n_chunk = 4
    phases = reduce_phases(n_line, n_tile)
    n_gram = sum(len(phase_peers(ph, n_line)) for ph in phases)
    n_steps = sum(reach - 1 for _, reach in scan_strides(n_point))
    field = pltpu.VMEM((n_comp, n_cols, n_point), jnp.float32)
    dma = pltpu.SemaphoreType.DMA
    f32 = jnp.float32
    inputs = (forcing.reshape(n_comp, n_cols, n_point), block_inverse, wall_rates, span_couple)
    out = pl.pallas_call(
        functools.partial(kernel, n_line, n_tile, n_chunk, phases, scale_value),
        out_shape=pltpu.VMEM((n_comp, n_cols, n_point), f32),
        in_specs=[pl.BlockSpec(memory_space=pltpu.HBM)] * 4,
        out_specs=pl.BlockSpec(memory_space=pltpu.VMEM),
        scratch_shapes=[
            field,
            pltpu.VMEM(block_inverse.shape, f32),
            pltpu.VMEM(wall_rates.shape, f32),
            pltpu.SMEM(span_couple.shape, f32),
            dma((4,)),
        ]
        + [field] * 7
        + [
            pltpu.VMEM((n_cols, n_point), f32),
            pltpu.VMEM((n_cols, n_point), f32),
            pltpu.VMEM((2, n_cols, n_point), f32),
            pltpu.VMEM((2, n_line - 1, n_cols, n_point), f32),
            pltpu.VMEM((n_cols, n_point), f32),
            pltpu.VMEM((2, ROWS, n_point), f32),
            pltpu.VMEM((n_line - 1, 2, ROWS, n_point), f32),
            pltpu.VMEM((2, n_steps, n_comp, 1, n_point), f32),
            pltpu.VMEM((2, n_comp, 1, n_point), f32),
            pltpu.VMEM((len(phases), n_cols // 2, 2 * n_cols), f32),
            pltpu.VMEM((n_gram, n_cols // 2, 2 * n_cols), f32),
            dma((2, n_chunk, 2)),
            dma((2, n_chunk, 2)),
            dma((n_chunk,)),
            dma((n_chunk,)),
            dma((2, n_chunk, n_line - 1)),
            dma((2, n_chunk, n_line - 1)),
            dma((n_line - 1,)),
            dma((n_line - 1,)),
            dma((n_gram,)),
            dma((n_gram,)),
        ],
        compiler_params=pltpu.CompilerParams(
            collective_id=0, has_side_effects=True, vmem_limit_bytes=32 * 1024 * 1024
        ),
    )(*[pltpu.with_memory_space_constraint(value, pltpu.HBM) for value in inputs])
    return out.reshape(n_comp, n_cols, 1, n_point)


def solution(mesh):
    in_specs = (
        P(None, None, "tile", "line"),
        P(None, None, "tile", "line"),
        P(None, None, "tile", "line"),
        P(),
    )
    out_specs = P(None, None, "tile", "line")
    return jax.shard_map(
        functools.partial(local, mesh.shape["line"], mesh.shape["tile"]),
        mesh=mesh, in_specs=in_specs, out_specs=out_specs, check_vma=False,
    )
```

```python
import functools
import math

import jax
import jax.numpy as jnp
from jax import lax
from jax.experimental import pallas as pl
from jax.experimental.pallas import tpu as pltpu
from jax.sharding import PartitionSpec as P

MESH = pl.DeviceIdType.MESH
ROWS = 8


def reduce_phases(n_line, n_tile):
    pair = 2 if n_tile % 2 == 0 else 1
    phases = [(1, pair, True)]
    stride, rest = pair, n_tile // pair
    while rest > 1:
        factor = 4 if rest % 4 == 0 else next(f for f in range(2, rest + 1) if rest % f == 0)
        phases.append((stride, factor, False))
        stride, rest = stride * factor, rest // factor
    return phases


def phase_peers(phase, n_line):
    stride, factor, with_line = phase
    lines = n_line if with_line else 1
    return [(a, b) for a in range(lines) for b in range(factor) if (a, b) != (0, 0)]


def peer_id(phase, step, n_line):
    stride, factor, _ = phase
    line, tile = lax.axis_index("line"), lax.axis_index("tile")
    digit = lax.rem(lax.div(tile, stride), factor)
    there = lax.rem(digit + step[1], factor)
    return (lax.rem(line + step[0], n_line), tile + (there - digit) * stride)


def scan_strides(n_point):
    strides, by = [], 1
    while by < n_point:
        reach = min(4, -(-n_point // by))
        strides.append((by, reach))
        by *= reach
    return strides


def split(value):
    high = value.astype(jnp.bfloat16)
    low = (value - high.astype(jnp.float32)).astype(jnp.bfloat16)
    return high, low


def eliminate(gram):
    n = gram.shape[0]
    row = lax.broadcasted_iota(jnp.int32, (n, n), 0)
    col = lax.broadcasted_iota(jnp.int32, (n, n), 1)
    both = jnp.concatenate([gram, (row == col).astype(jnp.float32)], axis=1)
    blocks = [both[v * ROWS : (v + 1) * ROWS] for v in range(n // ROWS)]
    shape = (ROWS, 2 * n)
    sub = lax.broadcasted_iota(jnp.int32, shape, 0)
    scales = []
    for q in range(n // ROWS):
        live = range(q, n // ROWS)
        cols = [
            {v: jnp.broadcast_to(blocks[v][:, ROWS * q + c : ROWS * q + c + 1], shape) for v in live}
            for c in range(ROWS)
        ]
        scale = jnp.zeros(shape, jnp.float32)
        for c in range(ROWS):
            pivot = jnp.broadcast_to(cols[c][q][c : c + 1], shape)
            inv = 1.0 / pivot
            scale = jnp.where(sub == c, lax.rsqrt(pivot), scale)
            factor = {v: cols[c][v] * inv for v in live}
            factor[q] = jnp.where(sub > c, factor[q], 0.0)
            top = jnp.broadcast_to(blocks[q][c : c + 1], shape)
            tops = [jnp.broadcast_to(cols[e][q][c : c + 1], shape) for e in range(c + 1, ROWS)]
            for v in live:
                blocks[v] = blocks[v] - factor[v] * top
                for e in range(c + 1, ROWS):
                    cols[e][v] = cols[e][v] - factor[v] * tops[e - c - 1]
        scales.append(scale)
    return jnp.concatenate([b * s for b, s in zip(blocks, scales)], axis=0)[:, n:]


def kernel(
    n_line, n_tile, n_chunk, phases, scale_value,
    f_in, a_in, w_in, s_in, o_ref,
    f_ref, a_ref, w_ref, s_ref, load_sem,
    start, z_low, z_high, rise, y_low, y_high, fall,
    edge_out, edge_in, ends_out, ends_in, enter, rates_out, rates_in, steps, whole,
    gram_out, gram_in, halo_send, halo_recv, edge_send, edge_recv, ends_send, ends_recv,
    rates_send, rates_recv, gram_send, gram_recv,
):
    loads = [
        pltpu.make_async_copy(src, dst, load_sem.at[i])
        for i, (src, dst) in enumerate(
            ((f_in, f_ref), (a_in, a_ref), (w_in, w_ref), (s_in, s_ref))
        )
    ]
    for load in loads:
        load.start()
    n_comp, n_cols, n_point = f_ref.shape
    wide = n_cols // n_chunk
    line, tile = lax.axis_index("line"), lax.axis_index("tile")
    above, below = lax.rem(tile + 1, n_tile), lax.rem(tile + n_tile - 1, n_tile)
    line_peers = [(lax.rem(line + d, n_line), tile) for d in range(1, n_line)]
    lower_line = (lax.rem(line + n_line - 1, n_line), tile)
    gram_peers = [[peer_id(ph, step, n_line) for step in phase_peers(ph, n_line)] for ph in phases]

    ends_in[...] = jnp.zeros(ends_in.shape, jnp.float32)
    greet = [(line, above), (line, below)] + [p for peers in gram_peers for p in peers]
    barrier = pltpu.get_barrier_semaphore()
    for peer in greet:
        pl.semaphore_signal(barrier, inc=1, device_id=peer, device_id_type=MESH)

    started = []

    def send(src, dst, send_sem, recv_sem, peer):
        copy = pltpu.make_async_remote_copy(
            src_ref=src, dst_ref=dst, send_sem=send_sem, recv_sem=recv_sem,
            device_id=peer, device_id_type=MESH,
        )
        copy.start()
        started.append(copy)
        return copy

    def cut(c):
        return pl.ds(pl.multiple_of(c * wide, wide), wide)

    lane3 = lax.broadcasted_iota(jnp.int32, (n_comp, 1, n_point), 2)
    lane8 = lax.broadcasted_iota(jnp.int32, (ROWS, n_point), 1)
    strides = scan_strides(n_point)

    def turn(value, by):
        flat = value.reshape(-1, n_point)
        return pltpu.roll(flat, by % n_point, 1).reshape(value.shape)

    def apply_block(value):
        total = a_ref[:, 0] * value[0][None]
        for m in range(1, n_comp):
            total = total + a_ref[:, m] * value[m][None]
        return total

    def pack(value, at):
        packed = jnp.zeros((value.shape[1], n_point), jnp.float32)
        places = lax.broadcasted_iota(jnp.int32, packed.shape, 1)
        for k in range(n_comp):
            packed = jnp.where(places == k, value[k][:, at : at + 1], packed)
        return packed

    def spread(packed):
        return jnp.stack(
            [jnp.broadcast_to(packed[:, k : k + 1], packed.shape) for k in range(n_comp)], axis=0
        )

    def sweep(value, side):
        slot = 0
        for by, reach in strides:
            parts = [turn(value, -by * m if side else by * m) for m in range(1, reach)]
            for part in parts:
                value = value + steps[side, slot] * part
                slot += 1
        return value

    rates = []

    def halo_copies(which, c):
        field, low, high = ((start, z_low, z_high), (rise, y_low, y_high))[which]
        return [
            pltpu.make_async_remote_copy(
                src_ref=field.at[:, cut(c)], dst_ref=there.at[:, cut(c)],
                send_sem=halo_send.at[which, c, side], recv_sem=halo_recv.at[which, c, side],
                device_id=(line, to), device_id_type=MESH,
            )
            for side, (there, to) in enumerate(((low, above), (high, below)))
        ]

    def edge_copy(c):
        return pltpu.make_async_remote_copy(
            src_ref=edge_out.at[cut(c)], dst_ref=edge_in.at[cut(c)], send_sem=edge_send.at[c],
            recv_sem=edge_recv.at[c], device_id=lower_line, device_id_type=MESH,
        )

    def ends_copy(which, c, d):
        return pltpu.make_async_remote_copy(
            src_ref=ends_out.at[which, cut(c)], dst_ref=ends_in.at[which, d, cut(c)],
            send_sem=ends_send.at[which, c, d], recv_sem=ends_recv.at[which, c, d],
            device_id=line_peers[d], device_id_type=MESH,
        )

    def reaches(which, d):
        if which:
            return line + d + 1 >= n_line, line + n_line - d - 1 < n_line
        return line + d + 1 < n_line, line >= d + 1

    def send_ends(which, c):
        for d in range(n_line - 1):
            @pl.when(reaches(which, d)[0])
            def _():
                ends_copy(which, c, d).start()

    def wait_ends(which, c, sent):
        for d in range(n_line - 1):
            @pl.when(reaches(which, d)[0 if sent else 1])
            def _():
                copy = ends_copy(which, c, d)
                copy.wait_send() if sent else copy.wait_recv()

    for load in loads:
        load.wait()
    def begin(c, _):
        field = apply_block(f_ref[:, cut(c)])
        start[:, cut(c)] = field
        edge_out[cut(c)] = pack(field, 0)

        @pl.when(c == 0)
        def _():
            pl.semaphore_wait(barrier, len(greet))

        for copy in halo_copies(0, c) + [edge_copy(c)]:
            copy.start()
        return 0

    lax.fori_loop(0, n_chunk, begin, 0)

    for side in range(2):
        rate = w_ref[side]
        slot = 0
        for by, reach in strides:
            parts = [rate]
            for m in range(1, reach):
                inside = lane3 < n_point - by * m if side else lane3 >= by * m
                steps[side, slot] = jnp.where(inside, rate, 0.0)
                slot += 1
                rate = rate * jnp.where(inside, turn(parts[0], -by * m if side else by * m), 1.0)
        whole[side] = rate
        at = 0 if side else n_point - 1
        total = jnp.zeros((ROWS, n_point), jnp.float32)
        for k in range(n_comp):
            total = jnp.where(lane8 == k, rate[k][:, at : at + 1], total)
        rates_out[side] = total
    for d, peer in enumerate(line_peers):
        rates.append(send(rates_out, rates_in.at[d], rates_send.at[d], rates_recv.at[d], peer))

    def coupled(c, low, high):
        beside = low[:, cut(c)] + high[:, cut(c)]
        return jnp.stack(
            [f_ref[k, cut(c)] + s_ref[k] * beside[k] for k in range(n_comp)], axis=0
        )

    def entry(which, c):
        wait_ends(which, c, False)
        total = jnp.zeros((wide, n_point), jnp.float32)
        carried = jnp.ones((1, n_point), jnp.float32)
        for d in range(1, n_line):
            slot = n_line - d - 1 if which else d - 1
            total = total + carried * ends_in[which, slot, cut(c)]
            carried = carried * rates_in[slot, which, 0:1]
        return total

    def first(c):
        for copy in halo_copies(0, c) + [edge_copy(c)]:
            copy.wait_recv()
        source = apply_block(coupled(c, z_low, z_high))
        last = (line < n_line - 1).astype(jnp.float32)
        over = jnp.where(
            lane3 == n_point - 1, spread(edge_in[cut(c)] * last),
            turn(start[:, cut(c)], -1),
        )
        value = sweep(source + w_ref[1] * over, 0)
        rise[:, cut(c)] = value
        ends_out[0, cut(c)] = pack(value, n_point - 1)
        send_ends(0, c)

    def first_entry(c):
        @pl.when(c == 0)
        def _():
            for copy in rates:
                copy.wait_recv()

        total = entry(0, c)
        enter[cut(c)] = total
        rise[:, cut(c)] = rise[:, cut(c)] + whole[0] * spread(total)
        for copy in halo_copies(1, c):
            copy.start()

    def second(c):
        for copy in halo_copies(1, c):
            copy.wait_recv()
        source = apply_block(coupled(c, y_low, y_high))
        under = jnp.where(
            lane3 == 0, spread(enter[cut(c)]), turn(rise[:, cut(c)], 1)
        )
        value = sweep(source + w_ref[0] * under, 1)
        fall[:, cut(c)] = value
        ends_out[1, cut(c)] = pack(value, 0)
        send_ends(1, c)

    def second_entry(c):
        fall[:, cut(c)] = fall[:, cut(c)] + whole[1] * spread(entry(1, c))

    def sweeps(work, finish):
        def step(c, _):
            @pl.when(c < n_chunk)
            def _():
                work(c)

            @pl.when(c > 0)
            def _():
                finish(c - 1)

            return 0

        lax.fori_loop(0, n_chunk + 1, step, 0)

    sweeps(first, first_entry)
    sweeps(second, second_entry)

    def drain(c, _):
        for copy in halo_copies(0, c) + halo_copies(1, c) + [edge_copy(c)]:
            copy.wait_send()
        for side in range(2):
            wait_ends(side, c, True)
        return 0

    total = jnp.zeros((2 * n_cols, 2 * n_cols), jnp.float32)
    for k in range(n_comp):
        both = jnp.concatenate(split(fall[k]), axis=0)
        total = total + lax.dot_general(
            both, both, (((1,), (1,)), ((), ())), preferred_element_type=jnp.float32
        )
    gram = total[:n_cols] + total[n_cols:]
    gram = gram[:, :n_cols] + gram[:, n_cols:]
    half = n_cols // 2
    packed = jnp.concatenate([gram[:half], gram[half:]], axis=1)
    slot = 0
    for i, peers in enumerate(gram_peers):
        gram_out[i] = packed
        copies = []
        for peer in peers:
            copies.append(
                send(gram_out.at[i], gram_in.at[slot], gram_send.at[slot], gram_recv.at[slot], peer)
            )
            slot += 1
        if i == 0:
            lax.fori_loop(0, n_chunk, drain, 0)
            for copy in rates:
                copy.wait_send()
        for j, copy in enumerate(copies):
            copy.wait_recv()
            packed = packed + gram_in[slot - len(copies) + j]
    gram = jnp.concatenate([packed[:, :n_cols], packed[:, n_cols:]], axis=0)

    high, low = split(eliminate(gram) * scale_value)
    left = jnp.concatenate([high, high, low], axis=1)
    for k in range(n_comp):
        top, rest = split(fall[k])
        o_ref[k] = jnp.dot(
            left, jnp.concatenate([top, rest, top], axis=0), preferred_element_type=jnp.float32
        )
    for copy in started[len(rates) :]:
        copy.wait_send()


def local(n_line, n_tile, forcing, block_inverse, wall_rates, span_couple):
    n_comp, n_cols, n_station, n_point = forcing.shape
    assert n_station == 1
    scale_value = math.sqrt(n_comp * n_station * n_tile * n_point * n_line)
    n_chunk = 2
    phases = reduce_phases(n_line, n_tile)
    n_gram = sum(len(phase_peers(ph, n_line)) for ph in phases)
    n_steps = sum(reach - 1 for _, reach in scan_strides(n_point))
    field = pltpu.VMEM((n_comp, n_cols, n_point), jnp.float32)
    dma = pltpu.SemaphoreType.DMA
    f32 = jnp.float32
    inputs = (forcing.reshape(n_comp, n_cols, n_point), block_inverse, wall_rates, span_couple)
    out = pl.pallas_call(
        functools.partial(kernel, n_line, n_tile, n_chunk, phases, scale_value),
        out_shape=pltpu.VMEM((n_comp, n_cols, n_point), f32),
        in_specs=[pl.BlockSpec(memory_space=pltpu.HBM)] * 4,
        out_specs=pl.BlockSpec(memory_space=pltpu.VMEM),
        scratch_shapes=[
            field,
            pltpu.VMEM(block_inverse.shape, f32),
            pltpu.VMEM(wall_rates.shape, f32),
            pltpu.SMEM(span_couple.shape, f32),
            dma((4,)),
        ]
        + [field] * 7
        + [
            pltpu.VMEM((n_cols, n_point), f32),
            pltpu.VMEM((n_cols, n_point), f32),
            pltpu.VMEM((2, n_cols, n_point), f32),
            pltpu.VMEM((2, n_line - 1, n_cols, n_point), f32),
            pltpu.VMEM((n_cols, n_point), f32),
            pltpu.VMEM((2, ROWS, n_point), f32),
            pltpu.VMEM((n_line - 1, 2, ROWS, n_point), f32),
            pltpu.VMEM((2, n_steps, n_comp, 1, n_point), f32),
            pltpu.VMEM((2, n_comp, 1, n_point), f32),
            pltpu.VMEM((len(phases), n_cols // 2, 2 * n_cols), f32),
            pltpu.VMEM((n_gram, n_cols // 2, 2 * n_cols), f32),
            dma((2, n_chunk, 2)),
            dma((2, n_chunk, 2)),
            dma((n_chunk,)),
            dma((n_chunk,)),
            dma((2, n_chunk, n_line - 1)),
            dma((2, n_chunk, n_line - 1)),
            dma((n_line - 1,)),
            dma((n_line - 1,)),
            dma((n_gram,)),
            dma((n_gram,)),
        ],
        compiler_params=pltpu.CompilerParams(
            collective_id=0, has_side_effects=True, vmem_limit_bytes=32 * 1024 * 1024
        ),
    )(*[pltpu.with_memory_space_constraint(value, pltpu.HBM) for value in inputs])
    return out.reshape(n_comp, n_cols, 1, n_point)


def solution(mesh):
    in_specs = (
        P(None, None, "tile", "line"),
        P(None, None, "tile", "line"),
        P(None, None, "tile", "line"),
        P(),
    )
    out_specs = P(None, None, "tile", "line")
    return jax.shard_map(
        functools.partial(local, mesh.shape["line"], mesh.shape["tile"]),
        mesh=mesh, in_specs=in_specs, out_specs=out_specs, check_vma=False,
    )
```

```python
import functools
import math

import jax
import jax.numpy as jnp
from jax import lax
from jax.experimental import pallas as pl
from jax.experimental.pallas import tpu as pltpu
from jax.sharding import PartitionSpec as P

MESH = pl.DeviceIdType.MESH
ROWS = 8


def reduce_phases(n_line, n_tile):
    pair = 2 if n_tile % 2 == 0 else 1
    phases = [(1, pair, True)]
    stride, rest = pair, n_tile // pair
    while rest > 1:
        factor = 4 if rest % 4 == 0 else next(f for f in range(2, rest + 1) if rest % f == 0)
        phases.append((stride, factor, False))
        stride, rest = stride * factor, rest // factor
    return phases


def phase_peers(phase, n_line):
    stride, factor, with_line = phase
    lines = n_line if with_line else 1
    return [(a, b) for a in range(lines) for b in range(factor) if (a, b) != (0, 0)]


def peer_id(phase, step, n_line):
    stride, factor, _ = phase
    line, tile = lax.axis_index("line"), lax.axis_index("tile")
    digit = lax.rem(lax.div(tile, stride), factor)
    there = lax.rem(digit + step[1], factor)
    return (lax.rem(line + step[0], n_line), tile + (there - digit) * stride)


def scan_strides(n_point):
    strides, by = [], 1
    while by < n_point:
        reach = min(4, -(-n_point // by))
        strides.append((by, reach))
        by *= reach
    return strides


def split(value):
    high = value.astype(jnp.bfloat16)
    low = (value - high.astype(jnp.float32)).astype(jnp.bfloat16)
    return high, low


def inverse_of(value):
    guess = pl.reciprocal(value, approx=True)
    guess = guess * (2.0 - value * guess)
    return guess * (2.0 - value * guess)


def eliminate(gram):
    n = gram.shape[0]
    row = lax.broadcasted_iota(jnp.int32, (n, n), 0)
    col = lax.broadcasted_iota(jnp.int32, (n, n), 1)
    both = jnp.concatenate([gram, (row == col).astype(jnp.float32)], axis=1)
    blocks = [both[v * ROWS : (v + 1) * ROWS] for v in range(n // ROWS)]
    shape = (ROWS, 2 * n)
    sub = lax.broadcasted_iota(jnp.int32, shape, 0)
    for q in range(n // ROWS):
        later = range(q + 1, n // ROWS)
        cols = [
            {
                v: jnp.broadcast_to(blocks[v][:, ROWS * q + c : ROWS * q + c + 1], shape)
                for v in range(q, n // ROWS)
            }
            for c in range(ROWS)
        ]
        cell = {
            (i, j): jnp.broadcast_to(cols[j][q][i : i + 1], shape)
            for i in range(ROWS) for j in range(i + 1)
        }
        lines = [jnp.broadcast_to(blocks[q][i : i + 1], shape) for i in range(ROWS)]
        for c in range(ROWS):
            inv = inverse_of(cell[c, c])
            for i in range(c + 1, ROWS):
                share = cell[i, c] * inv
                for j in range(c + 1, i + 1):
                    cell[i, j] = cell[i, j] - share * cell[j, c]
                lines[i] = lines[i] - share * lines[c]
            for v in later:
                share = cols[c][v] * inv
                blocks[v] = blocks[v] - share * lines[c]
                for e in range(c + 1, ROWS):
                    cols[e][v] = cols[e][v] - share * cell[e, c]
        done = lines[0] * lax.rsqrt(cell[0, 0])
        for i in range(1, ROWS):
            done = jnp.where(sub == i, lines[i] * lax.rsqrt(cell[i, i]), done)
        blocks[q] = done
    return jnp.concatenate(blocks, axis=0)[:, n:]


def kernel(
    n_line, n_tile, n_chunk, phases, scale_value,
    f_in, a_in, w_in, s_in, o_ref,
    f_ref, a_ref, w_ref, s_ref, load_sem,
    start, z_low, z_high, rise, y_low, y_high, fall,
    edge_out, edge_in, ends_out, ends_in, enter, rates_out, rates_in, steps, whole,
    gram_out, gram_in, halo_send, halo_recv, edge_send, edge_recv, ends_send, ends_recv,
    rates_send, rates_recv, gram_send, gram_recv,
):
    loads = [
        pltpu.make_async_copy(src, dst, load_sem.at[i])
        for i, (src, dst) in enumerate(
            ((f_in, f_ref), (a_in, a_ref), (w_in, w_ref), (s_in, s_ref))
        )
    ]
    for load in loads:
        load.start()
    n_comp, n_cols, n_point = f_ref.shape
    wide = n_cols // n_chunk
    line, tile = lax.axis_index("line"), lax.axis_index("tile")
    above, below = lax.rem(tile + 1, n_tile), lax.rem(tile + n_tile - 1, n_tile)
    line_peers = [(lax.rem(line + d, n_line), tile) for d in range(1, n_line)]
    lower_line = (lax.rem(line + n_line - 1, n_line), tile)
    gram_peers = [[peer_id(ph, step, n_line) for step in phase_peers(ph, n_line)] for ph in phases]

    ends_in[...] = jnp.zeros(ends_in.shape, jnp.float32)
    greet = [(line, above), (line, below)] + [p for peers in gram_peers for p in peers]
    barrier = pltpu.get_barrier_semaphore()
    for peer in greet:
        pl.semaphore_signal(barrier, inc=1, device_id=peer, device_id_type=MESH)

    started = []

    def send(src, dst, send_sem, recv_sem, peer):
        copy = pltpu.make_async_remote_copy(
            src_ref=src, dst_ref=dst, send_sem=send_sem, recv_sem=recv_sem,
            device_id=peer, device_id_type=MESH,
        )
        copy.start()
        started.append(copy)
        return copy

    def cut(c):
        return pl.ds(pl.multiple_of(c * wide, wide), wide)

    lane3 = lax.broadcasted_iota(jnp.int32, (n_comp, 1, n_point), 2)
    lane8 = lax.broadcasted_iota(jnp.int32, (ROWS, n_point), 1)
    strides = scan_strides(n_point)

    def turn(value, by):
        flat = value.reshape(-1, n_point)
        return pltpu.roll(flat, by % n_point, 1).reshape(value.shape)

    def apply_block(value):
        total = a_ref[:, 0] * value[0][None]
        for m in range(1, n_comp):
            total = total + a_ref[:, m] * value[m][None]
        return total

    def pack(value, at):
        packed = jnp.zeros((value.shape[1], n_point), jnp.float32)
        places = lax.broadcasted_iota(jnp.int32, packed.shape, 1)
        for k in range(n_comp):
            packed = jnp.where(places == k, value[k][:, at : at + 1], packed)
        return packed

    def spread(packed):
        return jnp.stack(
            [jnp.broadcast_to(packed[:, k : k + 1], packed.shape) for k in range(n_comp)], axis=0
        )

    def sweep(value, side):
        slot = 0
        for by, reach in strides:
            parts = [turn(value, -by * m if side else by * m) for m in range(1, reach)]
            for part in parts:
                value = value + steps[side, slot] * part
                slot += 1
        return value

    rates = []

    def halo_copies(which, c):
        field, low, high = ((start, z_low, z_high), (rise, y_low, y_high))[which]
        return [
            pltpu.make_async_remote_copy(
                src_ref=field.at[:, cut(c)], dst_ref=there.at[:, cut(c)],
                send_sem=halo_send.at[which, c, side], recv_sem=halo_recv.at[which, c, side],
                device_id=(line, to), device_id_type=MESH,
            )
            for side, (there, to) in enumerate(((low, above), (high, below)))
        ]

    def edge_copy(c):
        return pltpu.make_async_remote_copy(
            src_ref=edge_out.at[cut(c)], dst_ref=edge_in.at[cut(c)], send_sem=edge_send.at[c],
            recv_sem=edge_recv.at[c], device_id=lower_line, device_id_type=MESH,
        )

    def ends_copy(which, c, d):
        return pltpu.make_async_remote_copy(
            src_ref=ends_out.at[which, cut(c)], dst_ref=ends_in.at[which, d, cut(c)],
            send_sem=ends_send.at[which, c, d], recv_sem=ends_recv.at[which, c, d],
            device_id=line_peers[d], device_id_type=MESH,
        )

    def reaches(which, d):
        if which:
            return line + d + 1 >= n_line, line + n_line - d - 1 < n_line
        return line + d + 1 < n_line, line >= d + 1

    def send_ends(which, c):
        for d in range(n_line - 1):
            @pl.when(reaches(which, d)[0])
            def _():
                ends_copy(which, c, d).start()

    def wait_ends(which, c, sent):
        for d in range(n_line - 1):
            @pl.when(reaches(which, d)[0 if sent else 1])
            def _():
                copy = ends_copy(which, c, d)
                copy.wait_send() if sent else copy.wait_recv()

    for load in loads:
        load.wait()
    def begin(c, _):
        field = apply_block(f_ref[:, cut(c)])
        start[:, cut(c)] = field
        edge_out[cut(c)] = pack(field, 0)

        @pl.when(c == 0)
        def _():
            pl.semaphore_wait(barrier, len(greet))

        for copy in halo_copies(0, c) + [edge_copy(c)]:
            copy.start()
        return 0

    lax.fori_loop(0, n_chunk, begin, 0)

    for side in range(2):
        rate = w_ref[side]
        slot = 0
        for by, reach in strides:
            parts = [rate]
            for m in range(1, reach):
                inside = lane3 < n_point - by * m if side else lane3 >= by * m
                steps[side, slot] = jnp.where(inside, rate, 0.0)
                slot += 1
                rate = rate * jnp.where(inside, turn(parts[0], -by * m if side else by * m), 1.0)
        whole[side] = rate
        at = 0 if side else n_point - 1
        total = jnp.zeros((ROWS, n_point), jnp.float32)
        for k in range(n_comp):
            total = jnp.where(lane8 == k, rate[k][:, at : at + 1], total)
        rates_out[side] = total
    for d, peer in enumerate(line_peers):
        rates.append(send(rates_out, rates_in.at[d], rates_send.at[d], rates_recv.at[d], peer))

    def coupled(c, low, high):
        beside = low[:, cut(c)] + high[:, cut(c)]
        return jnp.stack(
            [f_ref[k, cut(c)] + s_ref[k] * beside[k] for k in range(n_comp)], axis=0
        )

    def entry(which, c):
        wait_ends(which, c, False)
        total = jnp.zeros((wide, n_point), jnp.float32)
        carried = jnp.ones((1, n_point), jnp.float32)
        for d in range(1, n_line):
            slot = n_line - d - 1 if which else d - 1
            total = total + carried * ends_in[which, slot, cut(c)]
            carried = carried * rates_in[slot, which, 0:1]
        return total

    def first(c):
        for copy in halo_copies(0, c) + [edge_copy(c)]:
            copy.wait_recv()
        source = apply_block(coupled(c, z_low, z_high))
        last = (line < n_line - 1).astype(jnp.float32)
        over = jnp.where(
            lane3 == n_point - 1, spread(edge_in[cut(c)] * last),
            turn(start[:, cut(c)], -1),
        )
        value = sweep(source + w_ref[1] * over, 0)
        rise[:, cut(c)] = value
        ends_out[0, cut(c)] = pack(value, n_point - 1)
        send_ends(0, c)

    def first_entry(c):
        @pl.when(c == 0)
        def _():
            for copy in rates:
                copy.wait_recv()

        total = entry(0, c)
        enter[cut(c)] = total
        rise[:, cut(c)] = rise[:, cut(c)] + whole[0] * spread(total)
        for copy in halo_copies(1, c):
            copy.start()

    def second(c):
        for copy in halo_copies(1, c):
            copy.wait_recv()
        source = apply_block(coupled(c, y_low, y_high))
        under = jnp.where(
            lane3 == 0, spread(enter[cut(c)]), turn(rise[:, cut(c)], 1)
        )
        value = sweep(source + w_ref[0] * under, 1)
        fall[:, cut(c)] = value
        ends_out[1, cut(c)] = pack(value, 0)
        send_ends(1, c)

    def second_entry(c):
        fall[:, cut(c)] = fall[:, cut(c)] + whole[1] * spread(entry(1, c))

    def sweeps(work, finish):
        def step(c, _):
            @pl.when(c < n_chunk)
            def _():
                work(c)

            @pl.when(c > 0)
            def _():
                finish(c - 1)

            return 0

        lax.fori_loop(0, n_chunk + 1, step, 0)

    sweeps(first, first_entry)
    sweeps(second, second_entry)

    def drain(c, _):
        for copy in halo_copies(0, c) + halo_copies(1, c) + [edge_copy(c)]:
            copy.wait_send()
        for side in range(2):
            wait_ends(side, c, True)
        return 0

    total = jnp.zeros((2 * n_cols, 2 * n_cols), jnp.float32)
    for k in range(n_comp):
        both = jnp.concatenate(split(fall[k]), axis=0)
        total = total + lax.dot_general(
            both, both, (((1,), (1,)), ((), ())), preferred_element_type=jnp.float32
        )
    gram = total[:n_cols] + total[n_cols:]
    gram = gram[:, :n_cols] + gram[:, n_cols:]
    half = n_cols // 2
    packed = jnp.concatenate([gram[:half], gram[half:]], axis=1)
    slot = 0
    for i, peers in enumerate(gram_peers):
        gram_out[i] = packed
        copies = []
        for peer in peers:
            copies.append(
                send(gram_out.at[i], gram_in.at[slot], gram_send.at[slot], gram_recv.at[slot], peer)
            )
            slot += 1
        if i == 0:
            lax.fori_loop(0, n_chunk, drain, 0)
            for copy in rates:
                copy.wait_send()
        for j, copy in enumerate(copies):
            copy.wait_recv()
            packed = packed + gram_in[slot - len(copies) + j]
    gram = jnp.concatenate([packed[:, :n_cols], packed[:, n_cols:]], axis=0)

    high, low = split(eliminate(gram) * scale_value)
    left = jnp.concatenate([high, high, low], axis=1)
    for k in range(n_comp):
        top, rest = split(fall[k])
        o_ref[k] = jnp.dot(
            left, jnp.concatenate([top, rest, top], axis=0), preferred_element_type=jnp.float32
        )
    for copy in started[len(rates) :]:
        copy.wait_send()


def local(n_line, n_tile, forcing, block_inverse, wall_rates, span_couple):
    n_comp, n_cols, n_station, n_point = forcing.shape
    assert n_station == 1
    scale_value = math.sqrt(n_comp * n_station * n_tile * n_point * n_line)
    n_chunk = 4
    phases = reduce_phases(n_line, n_tile)
    n_gram = sum(len(phase_peers(ph, n_line)) for ph in phases)
    n_steps = sum(reach - 1 for _, reach in scan_strides(n_point))
    field = pltpu.VMEM((n_comp, n_cols, n_point), jnp.float32)
    dma = pltpu.SemaphoreType.DMA
    f32 = jnp.float32
    inputs = (forcing.reshape(n_comp, n_cols, n_point), block_inverse, wall_rates, span_couple)
    out = pl.pallas_call(
        functools.partial(kernel, n_line, n_tile, n_chunk, phases, scale_value),
        out_shape=pltpu.VMEM((n_comp, n_cols, n_point), f32),
        in_specs=[pl.BlockSpec(memory_space=pltpu.HBM)] * 4,
        out_specs=pl.BlockSpec(memory_space=pltpu.VMEM),
        scratch_shapes=[
            field,
            pltpu.VMEM(block_inverse.shape, f32),
            pltpu.VMEM(wall_rates.shape, f32),
            pltpu.SMEM(span_couple.shape, f32),
            dma((4,)),
        ]
        + [field] * 7
        + [
            pltpu.VMEM((n_cols, n_point), f32),
            pltpu.VMEM((n_cols, n_point), f32),
            pltpu.VMEM((2, n_cols, n_point), f32),
            pltpu.VMEM((2, n_line - 1, n_cols, n_point), f32),
            pltpu.VMEM((n_cols, n_point), f32),
            pltpu.VMEM((2, ROWS, n_point), f32),
            pltpu.VMEM((n_line - 1, 2, ROWS, n_point), f32),
            pltpu.VMEM((2, n_steps, n_comp, 1, n_point), f32),
            pltpu.VMEM((2, n_comp, 1, n_point), f32),
            pltpu.VMEM((len(phases), n_cols // 2, 2 * n_cols), f32),
            pltpu.VMEM((n_gram, n_cols // 2, 2 * n_cols), f32),
            dma((2, n_chunk, 2)),
            dma((2, n_chunk, 2)),
            dma((n_chunk,)),
            dma((n_chunk,)),
            dma((2, n_chunk, n_line - 1)),
            dma((2, n_chunk, n_line - 1)),
            dma((n_line - 1,)),
            dma((n_line - 1,)),
            dma((n_gram,)),
            dma((n_gram,)),
        ],
        compiler_params=pltpu.CompilerParams(
            collective_id=0, has_side_effects=True, vmem_limit_bytes=32 * 1024 * 1024
        ),
    )(*[pltpu.with_memory_space_constraint(value, pltpu.HBM) for value in inputs])
    return out.reshape(n_comp, n_cols, 1, n_point)


def solution(mesh):
    in_specs = (
        P(None, None, "tile", "line"),
        P(None, None, "tile", "line"),
        P(None, None, "tile", "line"),
        P(),
    )
    out_specs = P(None, None, "tile", "line")
    return jax.shard_map(
        functools.partial(local, mesh.shape["line"], mesh.shape["tile"]),
        mesh=mesh, in_specs=in_specs, out_specs=out_specs, check_vma=False,
    )
```

```python
import functools
import math

import jax
import jax.numpy as jnp
from jax import lax
from jax.experimental import pallas as pl
from jax.experimental.pallas import tpu as pltpu
from jax.sharding import PartitionSpec as P

MESH = pl.DeviceIdType.MESH
ROWS = 8


def reduce_phases(n_line, n_tile):
    pair = 2 if n_tile % 2 == 0 else 1
    phases = [(1, pair, True)]
    stride, rest = pair, n_tile // pair
    while rest > 1:
        factor = 4 if rest % 4 == 0 else next(f for f in range(2, rest + 1) if rest % f == 0)
        phases.append((stride, factor, False))
        stride, rest = stride * factor, rest // factor
    return phases


def phase_peers(phase, n_line):
    stride, factor, with_line = phase
    lines = n_line if with_line else 1
    return [(a, b) for a in range(lines) for b in range(factor) if (a, b) != (0, 0)]


def peer_id(phase, step, n_line):
    stride, factor, _ = phase
    line, tile = lax.axis_index("line"), lax.axis_index("tile")
    digit = lax.rem(lax.div(tile, stride), factor)
    there = lax.rem(digit + step[1], factor)
    return (lax.rem(line + step[0], n_line), tile + (there - digit) * stride)


def scan_strides(n_point):
    strides, by = [], 1
    while by < n_point:
        reach = min(4, -(-n_point // by))
        strides.append((by, reach))
        by *= reach
    return strides


def split(value):
    high = value.astype(jnp.bfloat16)
    low = (value - high.astype(jnp.float32)).astype(jnp.bfloat16)
    return high, low


def eliminate(gram):
    n = gram.shape[0]
    row = lax.broadcasted_iota(jnp.int32, (n, n), 0)
    col = lax.broadcasted_iota(jnp.int32, (n, n), 1)
    both = jnp.concatenate([gram, (row == col).astype(jnp.float32)], axis=1)
    blocks = [both[v * ROWS : (v + 1) * ROWS] for v in range(n // ROWS)]
    shape = (ROWS, 2 * n)
    sub = lax.broadcasted_iota(jnp.int32, shape, 0)
    scales = []
    for q in range(n // ROWS):
        live = range(q, n // ROWS)
        cols = [
            {v: jnp.broadcast_to(blocks[v][:, ROWS * q + c : ROWS * q + c + 1], shape) for v in live}
            for c in range(ROWS)
        ]
        scale = jnp.zeros(shape, jnp.float32)
        for c in range(ROWS):
            pivot = jnp.broadcast_to(cols[c][q][c : c + 1], shape)
            inv = 1.0 / pivot
            scale = jnp.where(sub == c, lax.rsqrt(pivot), scale)
            factor = {v: cols[c][v] * inv for v in live}
            factor[q] = jnp.where(sub > c, factor[q], 0.0)
            top = jnp.broadcast_to(blocks[q][c : c + 1], shape)
            tops = [jnp.broadcast_to(cols[e][q][c : c + 1], shape) for e in range(c + 1, ROWS)]
            for v in live:
                blocks[v] = blocks[v] - factor[v] * top
                for e in range(c + 1, ROWS):
                    cols[e][v] = cols[e][v] - factor[v] * tops[e - c - 1]
        scales.append(scale)
    return jnp.concatenate([b * s for b, s in zip(blocks, scales)], axis=0)[:, n:]


def kernel(
    n_line, n_tile, n_chunk, phases, scale_value,
    f_in, a_in, w_in, s_in, o_ref,
    f_ref, a_ref, w_ref, s_ref, load_sem,
    start, z_low, z_high, rise, y_low, y_high, fall,
    edge_out, edge_in, ends_out, ends_in, enter, rates_out, rates_in, steps, whole,
    gram_out, gram_in, halo_send, halo_recv, edge_send, edge_recv, ends_send, ends_recv,
    rates_send, rates_recv, gram_send, gram_recv,
):
    loads = [
        pltpu.make_async_copy(src, dst, load_sem.at[i])
        for i, (src, dst) in enumerate(
            ((f_in, f_ref), (a_in, a_ref), (w_in, w_ref), (s_in, s_ref))
        )
    ]
    for load in loads:
        load.start()
    n_comp, n_cols, n_point = f_ref.shape
    wide = n_cols // n_chunk
    line, tile = lax.axis_index("line"), lax.axis_index("tile")
    above, below = lax.rem(tile + 1, n_tile), lax.rem(tile + n_tile - 1, n_tile)
    line_peers = [(lax.rem(line + d, n_line), tile) for d in range(1, n_line)]
    lower_line = (lax.rem(line + n_line - 1, n_line), tile)
    gram_peers = [[peer_id(ph, step, n_line) for step in phase_peers(ph, n_line)] for ph in phases]

    ends_in[...] = jnp.zeros(ends_in.shape, jnp.float32)
    greet = [(line, above), (line, below)] + [p for peers in gram_peers for p in peers]
    barrier = pltpu.get_barrier_semaphore()
    for peer in greet:
        pl.semaphore_signal(barrier, inc=1, device_id=peer, device_id_type=MESH)

    started = []

    def send(src, dst, send_sem, recv_sem, peer):
        copy = pltpu.make_async_remote_copy(
            src_ref=src, dst_ref=dst, send_sem=send_sem, recv_sem=recv_sem,
            device_id=peer, device_id_type=MESH,
        )
        copy.start()
        started.append(copy)
        return copy

    def cut(c):
        return pl.ds(pl.multiple_of(c * wide, wide), wide)

    lane3 = lax.broadcasted_iota(jnp.int32, (n_comp, 1, n_point), 2)
    lane8 = lax.broadcasted_iota(jnp.int32, (ROWS, n_point), 1)
    strides = scan_strides(n_point)

    def turn(value, by):
        flat = value.reshape(-1, n_point)
        return pltpu.roll(flat, by % n_point, 1).reshape(value.shape)

    def apply_block(value):
        total = a_ref[:, 0] * value[0][None]
        for m in range(1, n_comp):
            total = total + a_ref[:, m] * value[m][None]
        return total

    def pack(value, at):
        packed = jnp.zeros((value.shape[1], n_point), jnp.float32)
        places = lax.broadcasted_iota(jnp.int32, packed.shape, 1)
        for k in range(n_comp):
            packed = jnp.where(places == k, value[k][:, at : at + 1], packed)
        return packed

    def spread(packed):
        return jnp.stack(
            [jnp.broadcast_to(packed[:, k : k + 1], packed.shape) for k in range(n_comp)], axis=0
        )

    def sweep(value, side):
        slot = 0
        for by, reach in strides:
            parts = [turn(value, -by * m if side else by * m) for m in range(1, reach)]
            for part in parts:
                value = value + steps[side, slot] * part
                slot += 1
        return value

    rates = []

    def halo_copies(which, c):
        field, low, high = ((start, z_low, z_high), (rise, y_low, y_high))[which]
        return [
            pltpu.make_async_remote_copy(
                src_ref=field.at[:, cut(c)], dst_ref=there.at[:, cut(c)],
                send_sem=halo_send.at[which, c, side], recv_sem=halo_recv.at[which, c, side],
                device_id=(line, to), device_id_type=MESH,
            )
            for side, (there, to) in enumerate(((low, above), (high, below)))
        ]

    def edge_copy(c):
        return pltpu.make_async_remote_copy(
            src_ref=edge_out.at[cut(c)], dst_ref=edge_in.at[cut(c)], send_sem=edge_send.at[c],
            recv_sem=edge_recv.at[c], device_id=lower_line, device_id_type=MESH,
        )

    def ends_copy(which, c, d):
        return pltpu.make_async_remote_copy(
            src_ref=ends_out.at[which, cut(c)], dst_ref=ends_in.at[which, d, cut(c)],
            send_sem=ends_send.at[which, c, d], recv_sem=ends_recv.at[which, c, d],
            device_id=line_peers[d], device_id_type=MESH,
        )

    def reaches(which, d):
        if which:
            return line + d + 1 >= n_line, line + n_line - d - 1 < n_line
        return line + d + 1 < n_line, line >= d + 1

    def send_ends(which, c):
        for d in range(n_line - 1):
            @pl.when(reaches(which, d)[0])
            def _():
                ends_copy(which, c, d).start()

    def wait_ends(which, c, sent):
        for d in range(n_line - 1):
            @pl.when(reaches(which, d)[0 if sent else 1])
            def _():
                copy = ends_copy(which, c, d)
                copy.wait_send() if sent else copy.wait_recv()

    for load in loads:
        load.wait()
    def begin(c, _):
        field = apply_block(f_ref[:, cut(c)])
        start[:, cut(c)] = field
        edge_out[cut(c)] = pack(field, 0)

        @pl.when(c == 0)
        def _():
            pl.semaphore_wait(barrier, len(greet))

        for copy in halo_copies(0, c) + [edge_copy(c)]:
            copy.start()
        return 0

    lax.fori_loop(0, n_chunk, begin, 0)

    for side in range(2):
        rate = w_ref[side]
        slot = 0
        for by, reach in strides:
            parts = [rate]
            for m in range(1, reach):
                inside = lane3 < n_point - by * m if side else lane3 >= by * m
                steps[side, slot] = jnp.where(inside, rate, 0.0)
                slot += 1
                rate = rate * jnp.where(inside, turn(parts[0], -by * m if side else by * m), 1.0)
        whole[side] = rate
        at = 0 if side else n_point - 1
        total = jnp.zeros((ROWS, n_point), jnp.float32)
        for k in range(n_comp):
            total = jnp.where(lane8 == k, rate[k][:, at : at + 1], total)
        rates_out[side] = total
    for d, peer in enumerate(line_peers):
        rates.append(send(rates_out, rates_in.at[d], rates_send.at[d], rates_recv.at[d], peer))

    def coupled(c, low, high):
        beside = low[:, cut(c)] + high[:, cut(c)]
        return jnp.stack(
            [f_ref[k, cut(c)] + s_ref[k] * beside[k] for k in range(n_comp)], axis=0
        )

    def entry(which, c):
        wait_ends(which, c, False)
        total = jnp.zeros((wide, n_point), jnp.float32)
        carried = jnp.ones((1, n_point), jnp.float32)
        for d in range(1, n_line):
            slot = n_line - d - 1 if which else d - 1
            total = total + carried * ends_in[which, slot, cut(c)]
            carried = carried * rates_in[slot, which, 0:1]
        return total

    def first(c):
        for copy in halo_copies(0, c) + [edge_copy(c)]:
            copy.wait_recv()
        source = apply_block(coupled(c, z_low, z_high))
        last = (line < n_line - 1).astype(jnp.float32)
        over = jnp.where(
            lane3 == n_point - 1, spread(edge_in[cut(c)] * last),
            turn(start[:, cut(c)], -1),
        )
        value = sweep(source + w_ref[1] * over, 0)
        rise[:, cut(c)] = value
        ends_out[0, cut(c)] = pack(value, n_point - 1)
        send_ends(0, c)

    def first_entry(c):
        @pl.when(c == 0)
        def _():
            for copy in rates:
                copy.wait_recv()

        total = entry(0, c)
        enter[cut(c)] = total
        rise[:, cut(c)] = rise[:, cut(c)] + whole[0] * spread(total)
        for copy in halo_copies(1, c):
            copy.start()

    def second(c):
        for copy in halo_copies(1, c):
            copy.wait_recv()
        source = apply_block(coupled(c, y_low, y_high))
        under = jnp.where(
            lane3 == 0, spread(enter[cut(c)]), turn(rise[:, cut(c)], 1)
        )
        value = sweep(source + w_ref[0] * under, 1)
        fall[:, cut(c)] = value
        ends_out[1, cut(c)] = pack(value, 0)
        send_ends(1, c)

    def second_entry(c):
        fall[:, cut(c)] = fall[:, cut(c)] + whole[1] * spread(entry(1, c))

    def sweeps(work, finish):
        def step(c, _):
            @pl.when(c < n_chunk)
            def _():
                work(c)

            @pl.when(c > 0)
            def _():
                finish(c - 1)

            return 0

        lax.fori_loop(0, n_chunk + 1, step, 0)

    sweeps(first, first_entry)
    sweeps(second, second_entry)

    def drain(c, _):
        for copy in halo_copies(0, c) + halo_copies(1, c) + [edge_copy(c)]:
            copy.wait_send()
        for side in range(2):
            wait_ends(side, c, True)
        return 0

    total = jnp.zeros((2 * n_cols, 2 * n_cols), jnp.float32)
    for k in range(n_comp):
        both = jnp.concatenate(split(fall[k]), axis=0)
        total = total + lax.dot_general(
            both, both, (((1,), (1,)), ((), ())), preferred_element_type=jnp.float32
        )
    gram = total[:n_cols] + total[n_cols:]
    gram = gram[:, :n_cols] + gram[:, n_cols:]
    half = n_cols // 2
    packed = jnp.concatenate([gram[:half], gram[half:]], axis=1)
    slot = 0
    for i, peers in enumerate(gram_peers):
        gram_out[i] = packed
        copies = []
        for peer in peers:
            copies.append(
                send(gram_out.at[i], gram_in.at[slot], gram_send.at[slot], gram_recv.at[slot], peer)
            )
            slot += 1
        if i == 0:
            lax.fori_loop(0, n_chunk, drain, 0)
            for copy in rates:
                copy.wait_send()
        for j, copy in enumerate(copies):
            copy.wait_recv()
            packed = packed + gram_in[slot - len(copies) + j]
    gram = jnp.concatenate([packed[:, :n_cols], packed[:, n_cols:]], axis=0)

    high, low = split(eliminate(gram) * scale_value)
    left = jnp.concatenate([high, high, low], axis=1)
    for k in range(n_comp):
        top, rest = split(fall[k])
        o_ref[k] = jnp.dot(
            left, jnp.concatenate([top, rest, top], axis=0), preferred_element_type=jnp.float32
        )
    for copy in started[len(rates) :]:
        copy.wait_send()


def local(n_line, n_tile, forcing, block_inverse, wall_rates, span_couple):
    n_comp, n_cols, n_station, n_point = forcing.shape
    assert n_station == 1
    scale_value = math.sqrt(n_comp * n_station * n_tile * n_point * n_line)
    n_chunk = 8
    phases = reduce_phases(n_line, n_tile)
    n_gram = sum(len(phase_peers(ph, n_line)) for ph in phases)
    n_steps = sum(reach - 1 for _, reach in scan_strides(n_point))
    field = pltpu.VMEM((n_comp, n_cols, n_point), jnp.float32)
    dma = pltpu.SemaphoreType.DMA
    f32 = jnp.float32
    inputs = (forcing.reshape(n_comp, n_cols, n_point), block_inverse, wall_rates, span_couple)
    out = pl.pallas_call(
        functools.partial(kernel, n_line, n_tile, n_chunk, phases, scale_value),
        out_shape=pltpu.VMEM((n_comp, n_cols, n_point), f32),
        in_specs=[pl.BlockSpec(memory_space=pltpu.HBM)] * 4,
        out_specs=pl.BlockSpec(memory_space=pltpu.VMEM),
        scratch_shapes=[
            field,
            pltpu.VMEM(block_inverse.shape, f32),
            pltpu.VMEM(wall_rates.shape, f32),
            pltpu.SMEM(span_couple.shape, f32),
            dma((4,)),
        ]
        + [field] * 7
        + [
            pltpu.VMEM((n_cols, n_point), f32),
            pltpu.VMEM((n_cols, n_point), f32),
            pltpu.VMEM((2, n_cols, n_point), f32),
            pltpu.VMEM((2, n_line - 1, n_cols, n_point), f32),
            pltpu.VMEM((n_cols, n_point), f32),
            pltpu.VMEM((2, ROWS, n_point), f32),
            pltpu.VMEM((n_line - 1, 2, ROWS, n_point), f32),
            pltpu.VMEM((2, n_steps, n_comp, 1, n_point), f32),
            pltpu.VMEM((2, n_comp, 1, n_point), f32),
            pltpu.VMEM((len(phases), n_cols // 2, 2 * n_cols), f32),
            pltpu.VMEM((n_gram, n_cols // 2, 2 * n_cols), f32),
            dma((2, n_chunk, 2)),
            dma((2, n_chunk, 2)),
            dma((n_chunk,)),
            dma((n_chunk,)),
            dma((2, n_chunk, n_line - 1)),
            dma((2, n_chunk, n_line - 1)),
            dma((n_line - 1,)),
            dma((n_line - 1,)),
            dma((n_gram,)),
            dma((n_gram,)),
        ],
        compiler_params=pltpu.CompilerParams(
            collective_id=0, has_side_effects=True, vmem_limit_bytes=32 * 1024 * 1024
        ),
    )(*[pltpu.with_memory_space_constraint(value, pltpu.HBM) for value in inputs])
    return out.reshape(n_comp, n_cols, 1, n_point)


def solution(mesh):
    in_specs = (
        P(None, None, "tile", "line"),
        P(None, None, "tile", "line"),
        P(None, None, "tile", "line"),
        P(),
    )
    out_specs = P(None, None, "tile", "line")
    return jax.shard_map(
        functools.partial(local, mesh.shape["line"], mesh.shape["tile"]),
        mesh=mesh, in_specs=in_specs, out_specs=out_specs, check_vma=False,
    )
```
